512 devices in a mesh: texel: 32 (over x, y, core), light: 16 (over z).
Axes of the slice: x: 4, y: 4, z: 16, core: 2. Of those that a mesh axis runs over, the one named last changes fastest.
Arguments:
- tex_feat: bfloat16 [32768, 512], P('texel'), may hold values from -18 to 18
- light_feat: bfloat16 [24576, 512], P('light'), may hold values from -0.25 to 0.25
- sketch: bfloat16 [24576, 256], P('light'), may hold values from -0.0390625 to 0.0390625
- row_counts: int32 [32], replicated, may hold values from 1 to 1024, 16384 in all
Outputs:
- basis: float32 [32768, 256], P('texel')
- coeffs: float32 [256, 24576], P('texel', 'light')
The draws below stay inside these ranges and needn't reach their ends.
Inputs may be any that keep to these rules, and one draw needn't show every extreme that they name: row_counts sums to 32 * 512; some entry equals 1024.
All inputs are finite; a program needn't handle non-finite values.
Results may differ from the reference program's by a relative error of at most 0.0034.
Values sent between devices are 32-bit elements; how exact they have to be, the bound alone decides.
No kernel may reach another device: no remote copies, remote signals or barrier semaphores. Data moves between devices by JAX's collectives and lax.ppermute only.
A program may use at most 64 MiB of HBM per device.

```python
import math
import jax
import jax.numpy as jnp
import numpy as np
from jax import lax

F = 512
K = 256
CAP = 1024
LIGHT_DEV = 1536
TEX_SLOTS = 32768
LIGHTS = 24576
N_TEXEL = 32
N_LIGHT = 16


def level_of(key, extent, cuts, low, largest):
    def one(axis_at, parts):
        heights = jax.random.uniform(jax.random.fold_in(jax.random.fold_in(key, 6), axis_at), (parts,), jnp.float32, low / len(cuts), largest / len(cuts))
        return jnp.repeat(jnp.exp(heights), extent[axis_at] // parts).reshape((-1,) + (1,) * (len(extent) - axis_at - 1))

    factor_of = one(*cuts[0])
    for cut in cuts[1:]:
        factor_of = factor_of * one(*cut)
    return factor_of


def split_up(count, total, reach, slope):
    loads = [(1 << 20) // math.isqrt(grade ** slope) + 1 for grade in range(2, count + 1)]
    surplus, counts = total - reach - (count - 1), [1] * (count - 1)
    while surplus > 0:
        free = [i for i in range(count - 1) if counts[i] < reach]
        mass, remaining = sum([loads[i] for i in free]), surplus
        for i in free:
            extra = min(reach - counts[i], max(1, remaining * loads[i] // mass), surplus)
            counts[i] = counts[i] + extra
            surplus = surplus - extra
    return np.array([reach] + counts)


def ragged_sizes(own_key, amount, total, bound, slope):
    if amount == 2:
        one = jax.random.randint(own_key, (), max(1, total - bound), min(bound, total - 1) + 1)
        return jnp.stack([one, total - one])
    tallies = jnp.asarray(split_up(amount, total, bound, slope), jnp.int32)
    twos = (amount - 1) // 2
    source_of, sink = tallies[1:1 + 2 * twos:2], tallies[2:2 + 2 * twos:2]
    margin = jnp.minimum(source_of - 1, bound - sink)
    passed = jax.random.randint(jax.random.fold_in(own_key, 1), (twos,), 0, 1 << 20) % (margin + 1)
    tallies = tallies.at[1:1 + 2 * twos:2].set(source_of - passed).at[2:2 + 2 * twos:2].set(sink + passed)
    return tallies[jax.random.permutation(jax.random.fold_in(own_key, 2), amount)]


def scatter_about(key, dims, scale, limit, split=(), kind=jnp.bfloat16):
    factor_of = level_of(key, dims, split, -0.22, 0.18) if split else 1.0
    entries = jax.random.normal(key, dims, jnp.float32) * scale * factor_of
    return jnp.minimum(jnp.maximum(entries, -limit), limit).astype(kind)


def setup_inputs(seed: int = 0) -> dict:
    arg_keys = jax.random.split(jax.random.key(seed), 5)
    return {
        "tex_feat": scatter_about(arg_keys[0], (TEX_SLOTS, F), 3.0, 18.0, ((0, 32),)),
        "light_feat": scatter_about(arg_keys[1], (LIGHTS, F), F ** -0.5, 0.25, ((0, 16),)),
        "sketch": scatter_about(arg_keys[2], (LIGHTS, K), LIGHTS ** -0.5, 0.0390625, ((0, 16),)),
        "row_counts": ragged_sizes(arg_keys[3], N_TEXEL, N_TEXEL * CAP // 2, CAP, 2).astype(jnp.int32),
    }


def reference(tex_feat, light_feat, sketch, row_counts):
    slot_total = tex_feat.shape[0]
    positions = lax.iota(jnp.int32, slot_total)
    owners = (positions // CAP).astype(jnp.int32)
    row_valid = (positions % CAP < row_counts[owners]).astype(jnp.float32)
    valid_total = jnp.sum(row_counts).astype(jnp.float32)
    light_blocks = light_feat.reshape(N_LIGHT, LIGHT_DEV, F)
    sketch_blocks = sketch.reshape(N_LIGHT, LIGHT_DEV, K)

    def make_tiles(feats):
        logits = lax.dot_general(tex_feat.astype(jnp.float32), feats.astype(jnp.float32), (((1,), (1,)), ((), ())), preferred_element_type=jnp.float32)
        return jnp.sin(logits).astype(jnp.bfloat16)

    def accumulate(carry, pair):
        feats, block = pair
        return (carry + jnp.dot(make_tiles(feats).astype(jnp.float32), block.astype(jnp.float32), preferred_element_type=jnp.float32), None)
    sketched, _ = lax.scan(accumulate, jnp.zeros((slot_total, K), jnp.float32), (light_blocks, sketch_blocks))
    sketched = sketched * row_valid[:, None]
    gram_matrix = jnp.dot(sketched.T, sketched, precision=lax.Precision.HIGHEST) / valid_total
    factor = jnp.linalg.cholesky(gram_matrix)
    basis = jax.scipy.linalg.solve_triangular(factor, sketched.T, lower=True).T
    basis_half = basis.astype(jnp.bfloat16)

    def project(feats):
        return lax.dot_general(basis_half.astype(jnp.float32), make_tiles(feats).astype(jnp.float32), (((0,), (0,)), ((), ())), preferred_element_type=jnp.float32)
    coeff_blocks = lax.map(project, light_blocks)
    coeffs = jnp.transpose(coeff_blocks, (1, 0, 2)).reshape(K, N_LIGHT * LIGHT_DEV) / jnp.sqrt(valid_total)
    return (basis, coeffs)
```

```python
import math

import jax
import jax.numpy as jnp
import numpy as np
from jax import lax
from jax.experimental import pallas as pl
from jax.experimental.pallas import tpu as pltpu
from jax.sharding import Mesh, PartitionSpec as P

F32 = jnp.float32
BF16 = jnp.bfloat16
TEXEL = ("x", "y", "core")
FAR = ("z3", "z2", "z1")
LIGHT = FAR + ("z0",)
HIGHEST = lax.Precision.HIGHEST
VMEM_LIMIT = 48 * 2**20


def sine_coefficients():
    angle = (np.arange(4000) + 0.5) * math.pi / 4000
    u = 0.125 * (1 + np.cos(angle)) + 1e-9
    w = 1.0
    basis = np.stack([u ** (2 * i + 1) for i in range(5)], axis=1)
    fit, *_ = np.linalg.lstsq(basis / w, np.sin(2 * math.pi * u) / w, rcond=None)
    return [float(c) for c in fit]


SINE = sine_coefficients()
ROUNDER = float(1.5 * 2**23)


def sine(x):
    turns = x * F32(1 / (2 * math.pi))
    part = turns - ((turns + F32(ROUNDER)) - F32(ROUNDER))
    part = jnp.maximum(jnp.minimum(part, F32(0.5) - part), F32(-0.5) - part)
    sq = part * part
    value = F32(SINE[4])
    for c in SINE[3::-1]:
        value = value * sq + F32(c)
    return value * part


def dot(a, b, contract, precision=None):
    return lax.dot_general(
        a, b, ((contract[0:1], contract[1:2]), ((), ())), precision=precision, preferred_element_type=F32
    )


def tile_kernel(where_ref, counts_ref, tex_ref, light_ref, sketch_ref, tile_ref, part_ref, *, half, rows, blocks):
    first = (half + where_ref[1]) % 2 * (blocks * rows) + pl.program_id(0) * rows
    tile = sine(dot(tex_ref[...], light_ref[...], (1, 1))).astype(BF16)
    tile_ref[...] = tile
    part = dot(tile, sketch_ref[...], (1, 0))
    row = first + lax.broadcasted_iota(jnp.int32, part.shape, 0)
    part_ref[...] = jnp.where(row < counts_ref[where_ref[0]], part, 0.0)


def tile_call(half, where, counts, tex, light, sketch, rows=128):
    capacity, features = tex.shape
    lights, width = sketch.shape
    blocks = capacity // 2 // rows

    def tex_at(i, where_ref, counts_ref):
        return ((half + where_ref[1]) % 2 * blocks + i, 0)

    return pl.pallas_call(
        lambda *refs: tile_kernel(*refs, half=half, rows=rows, blocks=blocks),
        out_shape=(
            jax.ShapeDtypeStruct((capacity // 2, lights), BF16),
            jax.ShapeDtypeStruct((capacity // 2, width), F32),
        ),
        grid_spec=pltpu.PrefetchScalarGridSpec(
            num_scalar_prefetch=2,
            grid=(blocks,),
            in_specs=[
                pl.BlockSpec((rows, features), tex_at),
                pl.BlockSpec((lights, features), lambda i, *_: (0, 0)),
                pl.BlockSpec((lights, width), lambda i, *_: (0, 0)),
            ],
            out_specs=(
                pl.BlockSpec((rows, lights), lambda i, *_: (i, 0)),
                pl.BlockSpec((rows, width), lambda i, *_: (i, 0)),
            ),
        ),
        compiler_params=pltpu.CompilerParams(vmem_limit_bytes=VMEM_LIMIT),
        cost_estimate=pl.CostEstimate(
            flops=capacity * lights * (features + width), bytes_accessed=4 * 2**20, transcendentals=0
        ),
        name="tile_half",
    )(where, counts, tex, light, sketch)


def gram_kernel(own_ref, other_ref, gram_ref):
    gram_ref[...] = dot(own_ref[...], own_ref[...], (0, 0), HIGHEST) + dot(
        other_ref[...], other_ref[...], (0, 0), HIGHEST
    )


def invert_factor(gram, y_ref, a_ref, w_ref):
    size = gram.shape[0]
    row = lax.broadcasted_iota(jnp.int32, (size, size), 0)
    col = lax.broadcasted_iota(jnp.int32, (size, size), 1)
    diagonal = jnp.sum(jnp.where(row == col, gram, 0.0), axis=0, keepdims=True)
    a_ref[...] = gram
    y_ref[...] = jnp.where(row == col, lax.rsqrt(diagonal), 0.0)

    def refine(exact):
        precision = HIGHEST if exact else None
        cast = (lambda v: v) if exact else (lambda v: v.astype(BF16))
        y = cast(y_ref[...])
        product = dot(dot(y, cast(a_ref[...]), (1, 0), precision).astype(y.dtype), y, (1, 1), precision)
        off = product - jnp.where(row == col, F32(1), F32(0))
        step = jnp.where(row > col, off, jnp.where(row == col, 0.5 * off, 0.0))
        y_ref[...] = y_ref[...] - dot(cast(step), y, (1, 0), precision)
        return jnp.sum(off * off)

    def coarse(state):
        count, _ = state
        return count + 1, refine(False)

    def fine(state):
        count, _ = state
        return count + 1, refine(True)

    lax.while_loop(lambda s: (s[0] < 8) & (s[1] > 2e-2), coarse, (jnp.int32(0), F32(1)))
    _, rest = lax.while_loop(lambda s: (s[0] < 8) & (s[1] > 4e-6), fine, (jnp.int32(0), F32(1)))

    @pl.when(jnp.logical_not(rest <= 4e-6))
    def _():
        y_ref[...] = jnp.where(row == col, F32(1), F32(0))
        line = lax.broadcasted_iota(jnp.int32, (size, 1), 0)
        w_ref[...] = gram

        def eliminate(j, carry):
            work = w_ref[...]
            column = jnp.sum(jnp.where(col == j, work, 0.0), axis=1, keepdims=True)
            pivot = lax.rsqrt(jnp.sum(jnp.where(line == j, column, 0.0), axis=0, keepdims=True))
            top = w_ref[pl.ds(j, 1), :] * pivot
            top_y = y_ref[pl.ds(j, 1), :] * pivot
            factor = jnp.where(line > j, column * pivot, 0.0)
            w_ref[...] = work - factor * top
            y_ref[...] = jnp.where(line == j, top_y, y_ref[...] - factor * top_y)
            return carry

        lax.fori_loop(0, size, eliminate, 0)


def basis_kernel(
    where_ref, counts_ref, gram_ref, own_ref, other_ref, tile_own_ref, tile_other_ref,
    basis_ref, keep_ref, send_ref, y_ref, a_ref, w_ref, coeff_ref,
):
    total = F32(0)
    for i in range(counts_ref.shape[0]):
        total = total + counts_ref[i].astype(F32)
    gram = gram_ref[...] / total
    invert_factor(gram, y_ref, a_ref, w_ref)
    inverse = y_ref[...]
    half = own_ref.shape[0]
    own = dot(own_ref[...], inverse, (1, 1), HIGHEST)
    other = dot(other_ref[...], inverse, (1, 1), HIGHEST)
    parity = where_ref[1]
    basis_ref[pl.ds(pl.multiple_of(parity * half, half), half), :] = own
    basis_ref[pl.ds(pl.multiple_of((1 - parity) * half, half), half), :] = other
    coeffs = dot(own.astype(BF16), tile_own_ref[...], (0, 0)) + dot(other.astype(BF16), tile_other_ref[...], (0, 0))
    scale = 1.0 / jnp.sqrt(jnp.full((1, 1), total, F32))
    coeff_ref[...] = (coeffs * scale).reshape(coeff_ref.shape)
    core = where_ref[2]
    for i in range(keep_ref.shape[0]):
        keep_ref[i] = coeff_ref[2 * i + core]
        send_ref[i] = coeff_ref[2 * i + 1 - core]


def core_pairs():
    return [(i, i ^ 1) for i in range(2)]


def light_pairs(count):
    pairs = []
    for core in range(2):
        for z in range(count):
            other = z ^ 1 if core == 0 else ((((z - 1) % count) ^ 1) + 1) % count
            pairs.append((core * count + z, core * count + other))
    return pairs


def with_neighbour(value):
    return lax.ppermute(value, ("core", *LIGHT), light_pairs(lax.axis_size(LIGHT)))


def each_to_each(parts, axes):
    return lax.all_to_all(parts, axes, 0, 0, tiled=True)


def on_device(tex_feat, light_feat, sketch, row_counts):
    capacity, width = tex_feat.shape[0], sketch.shape[1]
    lights = light_feat.shape[0]
    half = capacity // 2
    texels, far = lax.axis_size(TEXEL), lax.axis_size(FAR)
    where = jnp.stack([lax.axis_index(TEXEL), lax.axis_index("z0"), lax.axis_index("core")]).astype(jnp.int32)

    tile_other, part_other = tile_call(1, where, row_counts, tex_feat, light_feat, sketch)
    arrived = with_neighbour(part_other)
    tile_own, part_own = tile_call(0, where, row_counts, tex_feat, light_feat, sketch)
    shares = each_to_each((part_own + arrived).reshape(far, half // far, width), FAR)
    share = jnp.sum(shares, axis=0)
    sketched_own = lax.all_gather(share, FAR, axis=0, tiled=True)
    sketched_other = with_neighbour(sketched_own)

    gram_part = pl.pallas_call(
        gram_kernel,
        out_shape=jax.ShapeDtypeStruct((width, width), F32),
        compiler_params=pltpu.CompilerParams(vmem_limit_bytes=VMEM_LIMIT),
        name="gram_part",
    )(sketched_own, sketched_other)
    gram_rows = jnp.sum(each_to_each(gram_part.reshape(texels, width // texels, width), TEXEL), axis=0)
    gram = each_to_each(jnp.broadcast_to(gram_rows, (texels, *gram_rows.shape)), TEXEL).reshape(width, width)

    lines = width // texels
    smem, vmem = pl.BlockSpec(memory_space=pltpu.SMEM), pl.BlockSpec(memory_space=pltpu.VMEM)
    basis, keep, send = pl.pallas_call(
        basis_kernel,
        out_shape=(
            jax.ShapeDtypeStruct((capacity, width), F32),
            jax.ShapeDtypeStruct((texels // 2, lines, lights), F32),
            jax.ShapeDtypeStruct((texels // 2, lines, lights), F32),
        ),
        in_specs=[smem, smem] + [vmem] * 5,
        out_specs=(vmem, vmem, vmem),
        scratch_shapes=[pltpu.VMEM((width, width), F32)] * 3 + [pltpu.VMEM((texels, lines, lights), F32)],
        compiler_params=pltpu.CompilerParams(vmem_limit_bytes=VMEM_LIMIT),
        name="basis_and_coeffs",
    )(where, row_counts, gram, sketched_own, sketched_other, tile_own, tile_other)
    mine = keep + lax.ppermute(send, "core", core_pairs())
    coeffs = jnp.sum(each_to_each(mine, ("x", "y")), axis=0)
    return basis, coeffs


def solution(mesh):
    fine = Mesh(np.asarray(mesh.devices).reshape(4, 4, 2, 2, 2, 2, 2), (*TEXEL, *LIGHT))
    placed = (P(TEXEL, None), P(LIGHT, None), P(LIGHT, None), P())
    return jax.shard_map(
        on_device, mesh=fine, in_specs=placed, out_specs=(P(TEXEL, None), P(TEXEL, LIGHT)), check_vma=False
    )
```

```python
import math

import jax
import jax.numpy as jnp
import numpy as np
from jax import lax
from jax.experimental import pallas as pl
from jax.experimental.pallas import tpu as pltpu
from jax.sharding import Mesh, PartitionSpec as P

F32 = jnp.float32
BF16 = jnp.bfloat16
TEXEL = ("x", "y", "core")
FAR = ("z3", "z2", "z1")
LIGHT = FAR + ("z0",)
HIGHEST = lax.Precision.HIGHEST
VMEM_LIMIT = 48 * 2**20


def sine_coefficients():
    angle = (np.arange(4000) + 0.5) * math.pi / 4000
    u = 0.125 * (1 + np.cos(angle)) + 1e-9
    w = 1.0
    basis = np.stack([u ** (2 * i + 1) for i in range(5)], axis=1)
    fit, *_ = np.linalg.lstsq(basis / w, np.sin(2 * math.pi * u) / w, rcond=None)
    return [float(c) for c in fit]


SINE = sine_coefficients()
ROUNDER = float(1.5 * 2**23)


def sine(x):
    turns = x * F32(1 / (2 * math.pi))
    part = turns - ((turns + F32(ROUNDER)) - F32(ROUNDER))
    part = jnp.maximum(jnp.minimum(part, F32(0.5) - part), F32(-0.5) - part)
    sq = part * part
    value = F32(SINE[4])
    for c in SINE[3::-1]:
        value = value * sq + F32(c)
    return value * part


def dot(a, b, contract, precision=None):
    return lax.dot_general(
        a, b, ((contract[0:1], contract[1:2]), ((), ())), precision=precision, preferred_element_type=F32
    )


def tile_kernel(
    where_ref, counts_ref, tex_ref, light_ref, sketch_ref, tile_ref, part_ref, *, half, rows, blocks, share
):
    parity, core, far = where_ref[1], where_ref[2], where_ref[3]
    step = pl.program_id(0)
    first = (half + parity) % 2 * (blocks * rows) + step * rows
    tile = sine(dot(tex_ref[...], light_ref[...], (1, 1))).astype(BF16)
    tile_ref[...] = tile
    part = dot(tile, sketch_ref[...], (1, 0))
    row = first + lax.broadcasted_iota(jnp.int32, part.shape, 0)
    part = jnp.where(row < counts_ref[where_ref[0]], part, 0.0)
    reference = (far + core * half) % 2
    shares = blocks * rows // share
    for i in range(rows // share):
        owner = step * (rows // share) + i
        place = (owner + reference) % 2 * (shares // 2) + owner // 2
        part_ref[pl.ds(pl.multiple_of(place * share, share), share), :] = part[i * share : (i + 1) * share, :]


def tile_call(half, where, counts, tex, light, sketch, share, rows=128):
    capacity, features = tex.shape
    lights, width = sketch.shape
    blocks = capacity // 2 // rows

    def tex_at(i, where_ref, counts_ref):
        return ((half + where_ref[1]) % 2 * blocks + i, 0)

    return pl.pallas_call(
        lambda *refs: tile_kernel(*refs, half=half, rows=rows, blocks=blocks, share=share),
        out_shape=(
            jax.ShapeDtypeStruct((capacity // 2, lights), BF16),
            jax.ShapeDtypeStruct((capacity // 2, width), F32),
        ),
        grid_spec=pltpu.PrefetchScalarGridSpec(
            num_scalar_prefetch=2,
            grid=(blocks,),
            in_specs=[
                pl.BlockSpec((rows, features), tex_at),
                pl.BlockSpec((lights, features), lambda i, *_: (0, 0)),
                pl.BlockSpec((lights, width), lambda i, *_: (0, 0)),
            ],
            out_specs=(
                pl.BlockSpec((rows, lights), lambda i, *_: (i, 0)),
                pl.BlockSpec((capacity // 2, width), lambda i, *_: (0, 0)),
            ),
        ),
        compiler_params=pltpu.CompilerParams(vmem_limit_bytes=VMEM_LIMIT),
        cost_estimate=pl.CostEstimate(
            flops=capacity * lights * (features + width), bytes_accessed=4 * 2**20, transcendentals=0
        ),
        name="tile_half",
    )(where, counts, tex, light, sketch)


def gram_kernel(shares_ref, share_ref, gram_ref):
    share = jnp.sum(shares_ref[...], axis=0)
    share_ref[...] = share
    gram_ref[...] = dot(share, share, (0, 0), HIGHEST)


def invert_factor(gram, y_ref, a_ref, w_ref):
    size = gram.shape[0]
    row = lax.broadcasted_iota(jnp.int32, (size, size), 0)
    col = lax.broadcasted_iota(jnp.int32, (size, size), 1)
    diagonal = jnp.sum(jnp.where(row == col, gram, 0.0), axis=0, keepdims=True)
    a_ref[...] = gram
    y_ref[...] = jnp.where(row == col, lax.rsqrt(diagonal), 0.0)

    def refine(exact):
        precision = HIGHEST if exact else None
        cast = (lambda v: v) if exact else (lambda v: v.astype(BF16))
        y = cast(y_ref[...])
        product = dot(dot(y, cast(a_ref[...]), (1, 0), precision).astype(y.dtype), y, (1, 1), precision)
        off = product - jnp.where(row == col, F32(1), F32(0))
        step = jnp.where(row > col, off, jnp.where(row == col, 0.5 * off, 0.0))
        y_ref[...] = y_ref[...] - dot(cast(step), y, (1, 0), precision)
        return jnp.sum(off * off)

    def coarse(state):
        count, _ = state
        return count + 1, refine(False)

    def fine(state):
        count, _ = state
        return count + 1, refine(True)

    lax.while_loop(lambda s: (s[0] < 8) & (s[1] > 2e-2), coarse, (jnp.int32(0), F32(1)))
    _, rest = lax.while_loop(lambda s: (s[0] < 8) & (s[1] > 4e-6), fine, (jnp.int32(0), F32(1)))

    @pl.when(jnp.logical_not(rest <= 4e-6))
    def _():
        y_ref[...] = jnp.where(row == col, F32(1), F32(0))
        line = lax.broadcasted_iota(jnp.int32, (size, 1), 0)
        w_ref[...] = gram

        def eliminate(j, carry):
            work = w_ref[...]
            column = jnp.sum(jnp.where(col == j, work, 0.0), axis=1, keepdims=True)
            pivot = lax.rsqrt(jnp.sum(jnp.where(line == j, column, 0.0), axis=0, keepdims=True))
            top = w_ref[pl.ds(j, 1), :] * pivot
            top_y = y_ref[pl.ds(j, 1), :] * pivot
            factor = jnp.where(line > j, column * pivot, 0.0)
            w_ref[...] = work - factor * top
            y_ref[...] = jnp.where(line == j, top_y, y_ref[...] - factor * top_y)
            return carry

        lax.fori_loop(0, size, eliminate, 0)


def inverse_kernel(counts_ref, gram_ref, inverse_ref, a_ref, w_ref):
    total = F32(0)
    for i in range(counts_ref.shape[0]):
        total = total + counts_ref[i].astype(F32)
    invert_factor(gram_ref[...] / total, inverse_ref, a_ref, w_ref)


def basis_kernel(
    where_ref, counts_ref, inverse_ref, own_ref, other_ref, tile_own_ref, tile_other_ref,
    basis_ref, keep_ref, send_ref, coeff_ref,
):
    total = F32(0)
    for i in range(counts_ref.shape[0]):
        total = total + counts_ref[i].astype(F32)
    inverse = inverse_ref[...]
    shares, share = own_ref.shape[0], own_ref.shape[1]
    half = shares * share
    parity, core, far = where_ref[1], where_ref[2], where_ref[3]
    near = (far + core * (2 * parity - 1) + shares) % shares
    coeffs = None
    for source_ref, tile_ref, side, place in (
        (own_ref, tile_own_ref, parity, far), (other_ref, tile_other_ref, 1 - parity, near)
    ):
        basis = dot(source_ref[...].reshape(half, source_ref.shape[2]), inverse, (1, 1), HIGHEST)
        for i in range(shares):
            apart = (i & 1) << 2 | i & 2 | i >> 2
            owner = ((((place + shares - core) % shares) ^ apart) + core) % shares
            at = pl.multiple_of(side * half + owner * share, share)
            basis_ref[pl.ds(at, share), :] = basis[i * share : (i + 1) * share, :]
        ordered = basis_ref[pl.ds(pl.multiple_of(side * half, half), half), :].astype(BF16)
        product = dot(ordered, tile_ref[...], (0, 0))
        coeffs = product if coeffs is None else coeffs + product
    scale = 1.0 / jnp.sqrt(jnp.full((1, 1), total, F32))
    coeff_ref[...] = (coeffs * scale).reshape(coeff_ref.shape)
    for i in range(keep_ref.shape[0]):
        keep_ref[i] = coeff_ref[2 * i + core]
        send_ref[i] = coeff_ref[2 * i + 1 - core]


def core_pairs():
    return [(i, i ^ 1) for i in range(2)]


def light_pairs(count, reach):
    pairs = []
    for core in range(2):
        shift = core * min(reach, 2)
        for z in range(count):
            pairs.append((core * count + z, core * count + ((((z - shift) % count) ^ reach) + shift) % count))
    return pairs


def across(value, reach):
    return lax.ppermute(value, ("core", *LIGHT), light_pairs(lax.axis_size(LIGHT), reach))


def each_to_each(parts, axes):
    return lax.all_to_all(parts, axes, 0, 0, tiled=True)


def to_each(value, axes):
    return each_to_each(jnp.broadcast_to(value, (lax.axis_size(axes), *value.shape)), axes)


def after(value, *others):
    return lax.optimization_barrier((value, *others))[0]


def on_device(tex_feat, light_feat, sketch, row_counts):
    capacity, width = tex_feat.shape[0], sketch.shape[1]
    lights = light_feat.shape[0]
    half = capacity // 2
    texels, far = lax.axis_size(TEXEL), lax.axis_size(FAR)
    share_rows = half // far
    places = [lax.axis_index(axes) for axes in (TEXEL, "z0", "core", FAR)]
    where = jnp.stack(places).astype(jnp.int32)

    inputs = (where, row_counts, tex_feat, light_feat, sketch, share_rows)
    tile_other, part_other = tile_call(1, *inputs)
    arrived = across(part_other, 1)
    tile_own, part_own = tile_call(0, *inputs)
    quarter = part_own[: half // 2] + arrived[: half // 2]
    quarter = quarter + across(part_own[half // 2 :] + arrived[half // 2 :], 2)
    shares = each_to_each(quarter.reshape(far // 2, share_rows, width), ("z3", "z2"))

    share, gram_part = pl.pallas_call(
        gram_kernel,
        out_shape=(jax.ShapeDtypeStruct((share_rows, width), F32), jax.ShapeDtypeStruct((width, width), F32)),
        compiler_params=pltpu.CompilerParams(vmem_limit_bytes=VMEM_LIMIT),
        name="gram_part",
    )(shares)

    held = share[None]
    held = jnp.concatenate([held, across(held, 8)])
    gram_rows = jnp.sum(each_to_each(gram_part.reshape(texels, width // texels, width), TEXEL), axis=0)
    held, gram_rows = lax.optimization_barrier((held, gram_rows))
    held = jnp.concatenate([held, across(held, 4)])
    gram_rows = jnp.sum(to_each(gram_rows, LIGHT), axis=0)
    held, gram_rows = lax.optimization_barrier((held, gram_rows))
    sketched_own = jnp.concatenate([held, across(held, 2)])
    gram = to_each(gram_rows, TEXEL).reshape(width, width)
    sketched_own, gram = lax.optimization_barrier((sketched_own, gram))
    sketched_other = across(sketched_own, 1)

    smem, vmem = pl.BlockSpec(memory_space=pltpu.SMEM), pl.BlockSpec(memory_space=pltpu.VMEM)
    inverse = pl.pallas_call(
        inverse_kernel,
        out_shape=jax.ShapeDtypeStruct((width, width), F32),
        in_specs=[smem, vmem],
        out_specs=vmem,
        scratch_shapes=[pltpu.VMEM((width, width), F32)] * 2,
        compiler_params=pltpu.CompilerParams(vmem_limit_bytes=VMEM_LIMIT),
        cost_estimate=pl.CostEstimate(flops=10**10, bytes_accessed=2**20, transcendentals=0),
        name="inverse_factor",
    )(row_counts, gram)

    lines = width // texels
    basis, keep, send = pl.pallas_call(
        basis_kernel,
        out_shape=(
            jax.ShapeDtypeStruct((capacity, width), F32),
            jax.ShapeDtypeStruct((texels // 2, lines, lights), F32),
            jax.ShapeDtypeStruct((texels // 2, lines, lights), F32),
        ),
        in_specs=[smem, smem] + [vmem] * 5,
        out_specs=(vmem, vmem, vmem),
        scratch_shapes=[pltpu.VMEM((texels, lines, lights), F32)],
        compiler_params=pltpu.CompilerParams(vmem_limit_bytes=VMEM_LIMIT),
        name="basis_and_coeffs",
    )(where, row_counts, inverse, sketched_own, sketched_other, tile_own, tile_other)
    mine = keep + lax.ppermute(send, "core", core_pairs())
    coeffs = jnp.sum(each_to_each(mine, ("x", "y")), axis=0)
    return basis, coeffs


def solution(mesh):
    fine = Mesh(np.asarray(mesh.devices).reshape(4, 4, 2, 2, 2, 2, 2), (*TEXEL, *LIGHT))
    placed = (P(TEXEL, None), P(LIGHT, None), P(LIGHT, None), P())
    return jax.shard_map(
        on_device, mesh=fine, in_specs=placed, out_specs=(P(TEXEL, None), P(TEXEL, LIGHT)), check_vma=False
    )
```

```python
import math

import jax
import jax.numpy as jnp
import numpy as np
from jax import lax
from jax.experimental import pallas as pl
from jax.experimental.pallas import tpu as pltpu
from jax.sharding import Mesh, PartitionSpec as P

F32 = jnp.float32
BF16 = jnp.bfloat16
CHIP = ("x", "y")
TEXEL = CHIP + ("core",)
LIGHT = ("z3", "z2", "z1", "z0")
HIGHEST = lax.Precision.HIGHEST
VMEM_LIMIT = 24 * 2**20


def sine_coefficients():
    angle = (np.arange(4000) + 0.5) * math.pi / 4000
    u = 0.125 * (1 + np.cos(angle)) + 1e-9
    w = 1.0
    basis = np.stack([u ** (2 * i + 1) for i in range(5)], axis=1)
    fit, *_ = np.linalg.lstsq(basis / w, np.sin(2 * math.pi * u) / w, rcond=None)
    return [float(c) for c in fit]


SINE = sine_coefficients()
ROUNDER = float(1.5 * 2**23)


def sine(x):
    turns = x * F32(1 / (2 * math.pi))
    part = turns - ((turns + F32(ROUNDER)) - F32(ROUNDER))
    part = jnp.maximum(jnp.minimum(part, F32(0.5) - part), F32(-0.5) - part)
    sq = part * part
    value = F32(SINE[4])
    for c in SINE[3::-1]:
        value = value * sq + F32(c)
    return value * part


def dot(a, b, contract, precision=None):
    return lax.dot_general(
        a, b, ((contract[0:1], contract[1:2]), ((), ())), precision=precision, preferred_element_type=F32
    )


def on_core(kernel, out_shape, in_specs, name, scratch=(), flops=10**9):
    vmem = pl.BlockSpec(memory_space=pltpu.VMEM)
    smem = pl.BlockSpec(memory_space=pltpu.SMEM)
    return pl.pallas_call(
        kernel,
        out_shape=out_shape,
        in_specs=[smem if spec else vmem for spec in in_specs],
        out_specs=jax.tree.map(lambda _: vmem, out_shape),
        scratch_shapes=scratch,
        compiler_params=pltpu.CompilerParams(vmem_limit_bytes=VMEM_LIMIT),
        cost_estimate=pl.CostEstimate(flops=flops, bytes_accessed=2**20, transcendentals=0),
        name=name,
    )


def quarter_of(order, where):
    low, second, core = where[1], where[2], where[3]
    if order < 2:
        return 2 * (1 - low) + (second + core + 1 - order) % 2
    return 2 * low + (second + 1 - (order - 2)) % 2


def tile_kernel(where_ref, counts_ref, tex_ref, light_ref, sketch_ref, tile_ref, part_ref, *, order, step=128):
    first = quarter_of(order, where_ref) * tile_ref.shape[0]
    count = counts_ref[where_ref[0]]
    for at in range(0, tile_ref.shape[0], step):
        tex = tex_ref[pl.ds(pl.multiple_of(first + at, step), step), :]
        tile = sine(dot(tex, light_ref[...], (1, 1))).astype(BF16)
        tile_ref[at : at + step, :] = tile
        part = dot(tile, sketch_ref[...], (1, 0))
        row = first + at + lax.broadcasted_iota(jnp.int32, part.shape, 0)
        part_ref[at : at + step, :] = jnp.where(row < count, part, 0.0)


def tile_call(order, where, counts, tex, light, sketch):
    rows = tex.shape[0] // 4
    return on_core(
        lambda *refs: tile_kernel(*refs, order=order),
        (
            jax.ShapeDtypeStruct((rows, light.shape[0]), BF16),
            jax.ShapeDtypeStruct((rows, sketch.shape[1]), F32),
        ),
        (True, True, False, False, False),
        "tile_quarter",
        flops=2 * rows * light.shape[0] * (tex.shape[1] + sketch.shape[1]),
    )(where, counts, tex, light, sketch)


def gram_kernel(most_ref, rest_ref, gram_ref):
    gram = None
    for ref in (most_ref, rest_ref):
        rows = ref[...].reshape(-1, ref.shape[-1])
        product = dot(rows, rows, (0, 0), HIGHEST)
        gram = product if gram is None else gram + product
    gram_ref[...] = gram


def invert_factor(gram, y_ref, a_ref, w_ref):
    size = gram.shape[0]
    row = lax.broadcasted_iota(jnp.int32, (size, size), 0)
    col = lax.broadcasted_iota(jnp.int32, (size, size), 1)
    diagonal = jnp.sum(jnp.where(row == col, gram, 0.0), axis=0, keepdims=True)
    a_ref[...] = gram
    y_ref[...] = jnp.where(row == col, lax.rsqrt(diagonal), 0.0)

    def refine(exact):
        precision = HIGHEST if exact else None
        cast = (lambda v: v) if exact else (lambda v: v.astype(BF16))
        y = cast(y_ref[...])
        product = dot(dot(y, cast(a_ref[...]), (1, 0), precision).astype(y.dtype), y, (1, 1), precision)
        off = product - jnp.where(row == col, F32(1), F32(0))
        step = jnp.where(row > col, off, jnp.where(row == col, 0.5 * off, 0.0))
        y_ref[...] = y_ref[...] - dot(cast(step), y, (1, 0), precision)
        return jnp.sum(off * off)

    def coarse(state):
        count, _ = state
        return count + 1, refine(False)

    def fine(state):
        count, _ = state
        return count + 1, refine(True)

    lax.while_loop(lambda s: (s[0] < 8) & (s[1] > 2e-2), coarse, (jnp.int32(0), F32(1)))
    _, rest = lax.while_loop(lambda s: (s[0] < 8) & (s[1] > 4e-6), fine, (jnp.int32(0), F32(1)))

    @pl.when(jnp.logical_not(rest <= 4e-6))
    def _():
        y_ref[...] = jnp.where(row == col, F32(1), F32(0))
        line = lax.broadcasted_iota(jnp.int32, (size, 1), 0)
        w_ref[...] = gram

        def eliminate(j, carry):
            work = w_ref[...]
            column = jnp.sum(jnp.where(col == j, work, 0.0), axis=1, keepdims=True)
            pivot = lax.rsqrt(jnp.sum(jnp.where(line == j, column, 0.0), axis=0, keepdims=True))
            top = w_ref[pl.ds(j, 1), :] * pivot
            top_y = y_ref[pl.ds(j, 1), :] * pivot
            factor = jnp.where(line > j, column * pivot, 0.0)
            w_ref[...] = work - factor * top
            y_ref[...] = jnp.where(line == j, top_y, y_ref[...] - factor * top_y)
            return carry

        lax.fori_loop(0, size, eliminate, 0)


def basis_kernel(
    where_ref, counts_ref, gram_ref, most_ref, rest_ref, *refs
):
    tile_refs, (basis_ref, keep_ref, send_ref, y_ref, a_ref, w_ref, coeff_ref) = refs[:4], refs[4:]
    total = F32(0)
    for i in range(counts_ref.shape[0]):
        total = total + counts_ref[i].astype(F32)
    invert_factor(gram_ref[...] / total, y_ref, a_ref, w_ref)
    inverse = y_ref[...]
    owners = most_ref.shape[0]
    share = most_ref.shape[1] + rest_ref.shape[1]
    quarter = owners * share // 4
    offset = 0
    for ref in (most_ref, rest_ref):
        lines = ref.shape[1]
        basis = dot(ref[...].reshape(owners * lines, ref.shape[2]), inverse, (1, 1), HIGHEST)
        for z in range(owners):
            start = (2 * (z & 1) + (z >> 1 & 1)) * quarter + (z >> 2) * share + offset
            basis_ref[start : start + lines, :] = basis[z * lines : (z + 1) * lines, :]
        offset += lines
    coeffs = None
    for order, tile_ref in enumerate(tile_refs):
        start = pl.multiple_of(quarter_of(order, where_ref) * quarter, quarter)
        product = dot(basis_ref[pl.ds(start, quarter), :].astype(BF16), tile_ref[...], (0, 0))
        coeffs = product if coeffs is None else coeffs + product
    scale = 1.0 / jnp.sqrt(jnp.full((1, 1), total, F32))
    coeff_ref[...] = (coeffs * scale).reshape(coeff_ref.shape)
    core = where_ref[3]
    for i in range(keep_ref.shape[0]):
        keep_ref[i] = coeff_ref[2 * i + core]
        send_ref[i] = coeff_ref[2 * i + 1 - core]


def light_pairs(count, reach):
    pairs = []
    for core in range(2):
        shift = core * reach
        for z in range(count):
            pairs.append((core * count + z, core * count + ((((z - shift) % count) ^ reach) + shift) % count))
    return pairs


def across(value, reach):
    return lax.ppermute(value, ("core", *LIGHT), light_pairs(lax.axis_size(LIGHT), reach))


def across_cores(value):
    return lax.ppermute(value, "core", [(0, 1), (1, 0)])


def each_to_each(parts, axes):
    return lax.all_to_all(parts, axes, 0, 0, tiled=True)


def to_each(value, axes):
    return each_to_each(jnp.broadcast_to(value, (lax.axis_size(axes), *value.shape)), axes)


def on_device(tex_feat, light_feat, sketch, row_counts):
    capacity, width = tex_feat.shape[0], sketch.shape[1]
    lights = light_feat.shape[0]
    texels, places = lax.axis_size(TEXEL), lax.axis_size(LIGHT)
    share = capacity // places
    most = share - 8
    where = jnp.stack([lax.axis_index(axes) for axes in (TEXEL, "z0", "z1", "core")]).astype(jnp.int32)

    inputs = (where, row_counts, tex_feat, light_feat, sketch)
    tiles, parts = [None] * 4, [None] * 4
    tiles[0], parts[0] = tile_call(0, *inputs)
    passing = across(parts[0], 1)
    tiles[1], parts[1] = tile_call(1, *inputs)
    staying = across(parts[1], 1)
    tiles[2], parts[2] = tile_call(2, *inputs)
    passed = across(parts[2] + passing, 2)
    tiles[3], parts[3] = tile_call(3, *inputs)
    quarter = parts[3] + staying + passed
    shares = each_to_each(quarter.reshape(places // 4, share, width), ("z3", "z2"))
    own = jnp.sum(shares, axis=0)

    rest_rows = to_each(own[most:], LIGHT)
    most_rows = lax.all_gather(own[:most], LIGHT, axis=0)
    rest_rows = rest_rows.reshape(places, share - most, width)

    gram = on_core(gram_kernel, jax.ShapeDtypeStruct((width, width), F32), (False, False), "gram_part")(
        most_rows, rest_rows
    )
    gram = gram + across_cores(gram)
    chips = lax.axis_size(CHIP)
    gram_rows = jnp.sum(each_to_each(gram.reshape(chips, width // chips, width), CHIP), axis=0)
    gram = to_each(gram_rows, CHIP).reshape(width, width)

    lines = width // texels
    basis, keep, send = on_core(
        basis_kernel,
        (
            jax.ShapeDtypeStruct((capacity, width), F32),
            jax.ShapeDtypeStruct((chips, lines, lights), F32),
            jax.ShapeDtypeStruct((chips, lines, lights), F32),
        ),
        (True, True) + (False,) * 7,
        "basis_and_coeffs",
        scratch=[pltpu.VMEM((width, width), F32)] * 3 + [pltpu.VMEM((texels, lines, lights), F32)],
    )(where, row_counts, gram, most_rows, rest_rows, *tiles)
    mine = keep + across_cores(send)
    coeffs = jnp.sum(each_to_each(mine, CHIP), axis=0)
    return basis, coeffs


def solution(mesh):
    fine = Mesh(np.asarray(mesh.devices).reshape(4, 4, 2, 2, 2, 2, 2), (*TEXEL, *LIGHT))
    placed = (P(TEXEL, None), P(LIGHT, None), P(LIGHT, None), P())
    return jax.shard_map(
        on_device, mesh=fine, in_specs=placed, out_specs=(P(TEXEL, None), P(TEXEL, LIGHT)), check_vma=False
    )
```

```python
import functools
import math

import jax
import jax.numpy as jnp
import numpy as np
from jax import lax
from jax.experimental import pallas as pl
from jax.experimental.pallas import tpu as pltpu
from jax.sharding import Mesh, PartitionSpec as P

F32 = jnp.float32
BF16 = jnp.bfloat16
CHIP = ("x", "y")
TEXEL = CHIP + ("core",)
FAR = ("z3", "z2")
LIGHT = FAR + ("z1", "z0")
HIGHEST = lax.Precision.HIGHEST
VMEM_LIMIT = 24 * 2**20
COUNTS = 5


def sine_coefficients():
    angle = (np.arange(4000) + 0.5) * math.pi / 4000
    u = 0.125 * (1 + np.cos(angle)) + 1e-9
    w = 1.0
    basis = np.stack([u ** (2 * i + 1) for i in range(5)], axis=1)
    fit, *_ = np.linalg.lstsq(basis / w, np.sin(2 * math.pi * u) / w, rcond=None)
    return [float(c) for c in fit]


SINE = sine_coefficients()
ROUNDER = float(1.5 * 2**23)


def sine(x):
    turns = x * F32(1 / (2 * math.pi))
    part = turns - ((turns + F32(ROUNDER)) - F32(ROUNDER))
    part = jnp.maximum(jnp.minimum(part, F32(0.5) - part), F32(-0.5) - part)
    sq = part * part
    value = F32(SINE[4])
    for c in SINE[3::-1]:
        value = value * sq + F32(c)
    return value * part


def dot(a, b, contract, precision=None):
    return lax.dot_general(
        a, b, ((contract[0:1], contract[1:2]), ((), ())), precision=precision, preferred_element_type=F32
    )


VMEM = pl.BlockSpec(memory_space=pltpu.VMEM)
SMEM = pl.BlockSpec(memory_space=pltpu.SMEM)


def on_core(kernel, out_shape, in_specs, name, scratch=(), flops=10**9, aliases=None):
    return pl.pallas_call(
        kernel,
        out_shape=out_shape,
        in_specs=in_specs,
        out_specs=jax.tree.map(lambda _: VMEM, out_shape),
        scratch_shapes=scratch,
        input_output_aliases=aliases or {},
        compiler_params=pltpu.CompilerParams(vmem_limit_bytes=VMEM_LIMIT),
        cost_estimate=pl.CostEstimate(flops=flops, bytes_accessed=2**20, transcendentals=0),
        name=name,
    )


def quarter_of(order, where):
    low, second, core = where[1], where[2], where[3]
    if order < 2:
        return 2 * (1 - low) + (second + core + 1 - order) % 2
    return 2 * low + (second + 1 - (order - 2)) % 2


def tile_kernel(where_ref, tex_ref, light_ref, sketch_ref, *refs, order, step=128):
    tile_ref, part_ref = refs[-2:]
    rows = part_ref.shape[0]
    first = quarter_of(order, where_ref) * rows
    count = where_ref[COUNTS + where_ref[0]]
    for at in range(0, rows, step):
        tex = tex_ref[pl.ds(pl.multiple_of(first + at, step), step), :]
        tile = sine(dot(tex, light_ref[...], (1, 1))).astype(BF16)
        tile_ref[order * rows + at : order * rows + at + step, :] = tile
        part = dot(tile, sketch_ref[...], (1, 0))
        row = first + at + lax.broadcasted_iota(jnp.int32, part.shape, 0)
        part_ref[at : at + step, :] = jnp.where(row < count, part, 0.0)


def tile_call(order, where, tex, light, sketch, *tiles):
    rows, lights, width = tex.shape[0] // 4, light.shape[0], sketch.shape[1]
    return on_core(
        lambda *refs: tile_kernel(*refs, order=order),
        (jax.ShapeDtypeStruct((tex.shape[0], lights), BF16), jax.ShapeDtypeStruct((rows, width), F32)),
        [SMEM] + [VMEM] * (3 + len(tiles)),
        "tile_quarter",
        flops=2 * rows * lights * (tex.shape[1] + width),
        aliases={4: 0} if tiles else None,
    )(where, tex, light, sketch, *tiles)


def gram_kernel(share_ref, gram_ref):
    gram_ref[...] = dot(share_ref[...], share_ref[...], (0, 0), HIGHEST)


def invert_factor(gram, y_ref, a_ref, w_ref):
    size = gram.shape[0]
    row = lax.broadcasted_iota(jnp.int32, (size, size), 0)
    col = lax.broadcasted_iota(jnp.int32, (size, size), 1)
    diagonal = jnp.sum(jnp.where(row == col, gram, 0.0), axis=0, keepdims=True)
    a_ref[...] = gram
    y_ref[...] = jnp.where(row == col, lax.rsqrt(diagonal), 0.0)

    def refine(exact):
        precision = HIGHEST if exact else None
        cast = (lambda v: v) if exact else (lambda v: v.astype(BF16))
        y = cast(y_ref[...])
        product = dot(dot(y, cast(a_ref[...]), (1, 0), precision).astype(y.dtype), y, (1, 1), precision)
        off = product - jnp.where(row == col, F32(1), F32(0))
        step = jnp.where(row > col, off, jnp.where(row == col, 0.5 * off, 0.0))
        y_ref[...] = y_ref[...] - dot(cast(step), y, (1, 0), precision)
        return jnp.sum(off * off)

    def coarse(state):
        count, _ = state
        return count + 1, refine(False)

    def fine(state):
        count, _ = state
        return count + 1, refine(True)

    lax.while_loop(lambda s: (s[0] < 8) & (s[1] > 2e-2), coarse, (jnp.int32(0), F32(1)))
    _, rest = lax.while_loop(lambda s: (s[0] < 8) & (s[1] > 4e-6), fine, (jnp.int32(0), F32(1)))

    @pl.when(jnp.logical_not(rest <= 4e-6))
    def _():
        y_ref[...] = jnp.where(row == col, F32(1), F32(0))
        line = lax.broadcasted_iota(jnp.int32, (size, 1), 0)
        w_ref[...] = gram

        def eliminate(j, carry):
            work = w_ref[...]
            column = jnp.sum(jnp.where(col == j, work, 0.0), axis=1, keepdims=True)
            pivot = lax.rsqrt(jnp.sum(jnp.where(line == j, column, 0.0), axis=0, keepdims=True))
            top = w_ref[pl.ds(j, 1), :] * pivot
            top_y = y_ref[pl.ds(j, 1), :] * pivot
            factor = jnp.where(line > j, column * pivot, 0.0)
            w_ref[...] = work - factor * top
            y_ref[...] = jnp.where(line == j, top_y, y_ref[...] - factor * top_y)
            return carry

        lax.fori_loop(0, size, eliminate, 0)


def total_of(where_ref):
    total = F32(0)
    for i in range(COUNTS, where_ref.shape[0]):
        total = total + where_ref[i].astype(F32)
    return total


def inverse_kernel(where_ref, gram_ref, inverse_ref, a_ref, w_ref):
    invert_factor(gram_ref[...] / total_of(where_ref), inverse_ref, a_ref, w_ref)


def basis_kernel(
    where_ref, inverse_ref, own_ref, other_ref, tile_ref,
    basis_ref, keep_ref, send_ref, half_ref, coeff_ref, *, share, places,
):
    inverse = inverse_ref[...]
    rows = basis_ref.shape[0] // 4
    groups = rows // share
    own, core = where_ref[4], where_ref[3]

    def partner(z, reach):
        shift = core * reach
        return (((z - shift + places) % places ^ reach) + shift) % places

    for ref, owner, orders in ((own_ref, own, (3, 2)), (other_ref, partner(own, 1), (1, 0))):
        basis = dot(ref[...], inverse, (1, 1), HIGHEST)
        for i, order in enumerate(orders):
            group = (owner if i == 0 else partner(owner, 2)) // (places // groups)
            start = quarter_of(order, where_ref) * rows
            for j, turn in enumerate((0, groups - 1, 1, 2)):
                at = (group + turn) % groups * share
                part = basis[i * rows + j * share : i * rows + (j + 1) * share, :]
                basis_ref[pl.ds(pl.multiple_of(start + at, share), share), :] = part
                half_ref[pl.ds(pl.multiple_of(order * rows + at, share), share), :] = part.astype(BF16)
    coeffs = dot(half_ref[...], tile_ref[...], (0, 0))
    scale = 1.0 / jnp.sqrt(jnp.full((1, 1), total_of(where_ref), F32))
    coeff_ref[...] = (coeffs * scale).reshape(coeff_ref.shape)
    for i in range(keep_ref.shape[0]):
        keep_ref[i] = coeff_ref[2 * i + core]
        send_ref[i] = coeff_ref[2 * i + 1 - core]


def light_pairs(count, reach):
    pairs = []
    for core in range(2):
        shift = core * reach
        for z in range(count):
            pairs.append((core * count + z, core * count + ((((z - shift) % count) ^ reach) + shift) % count))
    return pairs


def across(value, reach):
    return lax.ppermute(value, ("core", *LIGHT), light_pairs(lax.axis_size(LIGHT), reach))


def across_cores(value):
    return lax.ppermute(value, "core", [(0, 1), (1, 0)])


def each_to_each(parts, axes):
    return lax.all_to_all(parts, axes, 0, 0, tiled=True)


def to_each(value, axes):
    return each_to_each(jnp.broadcast_to(value, (lax.axis_size(axes), *value.shape)), axes)


def around(value, turn):
    places = lax.axis_size(LIGHT)
    return lax.ppermute(value, LIGHT, [(z, (z + 4 * turn) % places) for z in range(places)])


def on_device(tex_feat, light_feat, sketch, row_counts):
    capacity, width = tex_feat.shape[0], sketch.shape[1]
    lights = light_feat.shape[0]
    texels, places = lax.axis_size(TEXEL), lax.axis_size(LIGHT)
    share_rows = capacity // places
    marks = [lax.axis_index(axes) for axes in (TEXEL, "z0", "z1", "core", LIGHT)]
    where = jnp.concatenate([jnp.stack(marks).astype(jnp.int32), row_counts])

    inputs = (where, tex_feat, light_feat, sketch)
    tiles, part = tile_call(0, *inputs)
    passing = across(part, 1)
    tiles, part = tile_call(1, *inputs, tiles)
    staying = across(part, 1)
    tiles, part = tile_call(2, *inputs, tiles)
    passed = across(part + passing, 2)
    tiles, part = tile_call(3, *inputs, tiles)
    quarter = part + staying + passed
    share = jnp.sum(each_to_each(quarter.reshape(places // 4, share_rows, width), FAR), axis=0)

    before, behind = around(share, 1), around(share, -1)
    gram = on_core(gram_kernel, jax.ShapeDtypeStruct((width, width), F32), [VMEM], "gram_part")(share)
    gram_rows = jnp.sum(each_to_each(gram.reshape(texels, width // texels, width), TEXEL), axis=0)
    gram_rows, before, behind = lax.optimization_barrier((gram_rows, before, behind))
    opposite = around(before, 1)
    gram_rows = jnp.sum(to_each(gram_rows, LIGHT), axis=0)
    gram_rows, opposite = lax.optimization_barrier((gram_rows, opposite))
    quarter = jnp.concatenate([share, before, behind, opposite])
    own = jnp.concatenate([quarter, across(quarter, 2)])
    gram = to_each(gram_rows, TEXEL).reshape(width, width)
    gram, own = lax.optimization_barrier((gram, own))
    other = across(own, 1)
    inverse = on_core(
        inverse_kernel,
        jax.ShapeDtypeStruct((width, width), F32),
        [SMEM, VMEM],
        "inverse_factor",
        [pltpu.VMEM((width, width), F32)] * 2,
        10**10,
    )(where, gram)

    lines, chips = width // texels, lax.axis_size(CHIP)
    basis, keep, send = on_core(
        functools.partial(basis_kernel, share=share_rows, places=places),
        (
            jax.ShapeDtypeStruct((capacity, width), F32),
            jax.ShapeDtypeStruct((chips, lines, lights), F32),
            jax.ShapeDtypeStruct((chips, lines, lights), F32),
        ),
        [SMEM] + [VMEM] * 4,
        "basis_and_coeffs",
        [pltpu.VMEM((capacity, width), BF16), pltpu.VMEM((texels, lines, lights), F32)],
    )(where, inverse, own, other, tiles)
    mine = keep + across_cores(send)
    coeffs = jnp.sum(each_to_each(mine, CHIP), axis=0)
    return basis, coeffs


def solution(mesh):
    fine = Mesh(np.asarray(mesh.devices).reshape(4, 4, 2, 2, 2, 2, 2), (*TEXEL, *LIGHT))
    placed = (P(TEXEL, None), P(LIGHT, None), P(LIGHT, None), P())
    return jax.shard_map(
        on_device, mesh=fine, in_specs=placed, out_specs=(P(TEXEL, None), P(TEXEL, LIGHT)), check_vma=False
    )
```

```python
import math

import jax
import jax.numpy as jnp
import numpy as np
from jax import lax
from jax.experimental import pallas as pl
from jax.experimental.pallas import tpu as pltpu
from jax.sharding import Mesh, PartitionSpec as P

F32 = jnp.float32
BF16 = jnp.bfloat16
CHIP = ("x", "y")
TEXEL = CHIP + ("core",)
FAR = ("z3", "z2")
LIGHT = FAR + ("z1", "z0")
HIGHEST = lax.Precision.HIGHEST
VMEM_LIMIT = 24 * 2**20
COUNTS = 4


def sine_coefficients():
    angle = (np.arange(4000) + 0.5) * math.pi / 4000
    u = 0.125 * (1 + np.cos(angle)) + 1e-9
    w = 1.0
    basis = np.stack([u ** (2 * i + 1) for i in range(5)], axis=1)
    fit, *_ = np.linalg.lstsq(basis / w, np.sin(2 * math.pi * u) / w, rcond=None)
    return [float(c) for c in fit]


SINE = sine_coefficients()
ROUNDER = float(1.5 * 2**23)


def sine(x):
    turns = x * F32(1 / (2 * math.pi))
    part = turns - ((turns + F32(ROUNDER)) - F32(ROUNDER))
    part = jnp.maximum(jnp.minimum(part, F32(0.5) - part), F32(-0.5) - part)
    sq = part * part
    value = F32(SINE[4])
    for c in SINE[3::-1]:
        value = value * sq + F32(c)
    return value * part


def dot(a, b, contract, precision=None):
    return lax.dot_general(
        a, b, ((contract[0:1], contract[1:2]), ((), ())), precision=precision, preferred_element_type=F32
    )


VMEM = pl.BlockSpec(memory_space=pltpu.VMEM)
SMEM = pl.BlockSpec(memory_space=pltpu.SMEM)


def on_core(kernel, out_shape, in_specs, name, scratch=(), flops=10**9, aliases=None):
    return pl.pallas_call(
        kernel,
        out_shape=out_shape,
        in_specs=in_specs,
        out_specs=jax.tree.map(lambda _: VMEM, out_shape),
        scratch_shapes=scratch,
        input_output_aliases=aliases or {},
        compiler_params=pltpu.CompilerParams(vmem_limit_bytes=VMEM_LIMIT),
        cost_estimate=pl.CostEstimate(flops=flops, bytes_accessed=2**20, transcendentals=0),
        name=name,
    )


def quarter_of(order, where):
    low, second, core = where[1], where[2], where[3]
    if order < 2:
        return 2 * (1 - low) + (second + core + 1 - order) % 2
    return 2 * low + (second + 1 - (order - 2)) % 2


def tile_kernel(where_ref, tex_ref, light_ref, sketch_ref, *refs, order, step=128):
    tile_ref, part_ref = refs[-2:]
    rows = part_ref.shape[0]
    first = quarter_of(order, where_ref) * rows
    count = where_ref[COUNTS + where_ref[0]]
    for at in range(0, rows, step):
        tex = tex_ref[pl.ds(pl.multiple_of(first + at, step), step), :]
        tile = sine(dot(tex, light_ref[...], (1, 1))).astype(BF16)
        tile_ref[order * rows + at : order * rows + at + step, :] = tile
        part = dot(tile, sketch_ref[...], (1, 0))
        row = first + at + lax.broadcasted_iota(jnp.int32, part.shape, 0)
        part_ref[at : at + step, :] = jnp.where(row < count, part, 0.0)


def tile_call(order, where, tex, light, sketch, *tiles):
    rows, lights, width = tex.shape[0] // 4, light.shape[0], sketch.shape[1]
    return on_core(
        lambda *refs: tile_kernel(*refs, order=order),
        (jax.ShapeDtypeStruct((tex.shape[0], lights), BF16), jax.ShapeDtypeStruct((rows, width), F32)),
        [SMEM] + [VMEM] * (3 + len(tiles)),
        "tile_quarter",
        flops=2 * rows * lights * (tex.shape[1] + width),
        aliases={4: 0} if tiles else None,
    )(where, tex, light, sketch, *tiles)


def gram_kernel(share_ref, gram_ref):
    gram_ref[...] = dot(share_ref[...], share_ref[...], (0, 0), HIGHEST)


def invert_factor(gram, y_ref, a_ref, w_ref):
    size = gram.shape[0]
    row = lax.broadcasted_iota(jnp.int32, (size, size), 0)
    col = lax.broadcasted_iota(jnp.int32, (size, size), 1)
    diagonal = jnp.sum(jnp.where(row == col, gram, 0.0), axis=0, keepdims=True)
    a_ref[...] = gram
    y_ref[...] = jnp.where(row == col, lax.rsqrt(diagonal), 0.0)

    def refine(exact):
        precision = HIGHEST if exact else None
        cast = (lambda v: v) if exact else (lambda v: v.astype(BF16))
        y = cast(y_ref[...])
        product = dot(dot(y, cast(a_ref[...]), (1, 0), precision).astype(y.dtype), y, (1, 1), precision)
        off = product - jnp.where(row == col, F32(1), F32(0))
        step = jnp.where(row > col, off, jnp.where(row == col, 0.5 * off, 0.0))
        y_ref[...] = y_ref[...] - dot(cast(step), y, (1, 0), precision)
        return jnp.sum(off * off)

    def coarse(state):
        count, _ = state
        return count + 1, refine(False)

    def fine(state):
        count, _ = state
        return count + 1, refine(True)

    lax.while_loop(lambda s: (s[0] < 8) & (s[1] > 2e-2), coarse, (jnp.int32(0), F32(1)))
    _, rest = lax.while_loop(lambda s: (s[0] < 8) & (s[1] > 4e-6), fine, (jnp.int32(0), F32(1)))

    @pl.when(jnp.logical_not(rest <= 4e-6))
    def _():
        y_ref[...] = jnp.where(row == col, F32(1), F32(0))
        line = lax.broadcasted_iota(jnp.int32, (size, 1), 0)
        w_ref[...] = gram

        def eliminate(j, carry):
            work = w_ref[...]
            column = jnp.sum(jnp.where(col == j, work, 0.0), axis=1, keepdims=True)
            pivot = lax.rsqrt(jnp.sum(jnp.where(line == j, column, 0.0), axis=0, keepdims=True))
            top = w_ref[pl.ds(j, 1), :] * pivot
            top_y = y_ref[pl.ds(j, 1), :] * pivot
            factor = jnp.where(line > j, column * pivot, 0.0)
            w_ref[...] = work - factor * top
            y_ref[...] = jnp.where(line == j, top_y, y_ref[...] - factor * top_y)
            return carry

        lax.fori_loop(0, size, eliminate, 0)


def total_of(where_ref):
    total = F32(0)
    for i in range(COUNTS, where_ref.shape[0]):
        total = total + where_ref[i].astype(F32)
    return total


def inverse_kernel(where_ref, gram_ref, inverse_ref, a_ref, w_ref):
    invert_factor(gram_ref[...] / total_of(where_ref), inverse_ref, a_ref, w_ref)


def basis_kernel(
    where_ref, inverse_ref, gathered_ref, tile_ref, basis_ref, keep_ref, send_ref, half_ref, coeff_ref
):
    pairs, two, share = gathered_ref.shape[:3]
    low, second, core = where_ref[1], where_ref[2], where_ref[3]
    rows = basis_ref.shape[0] // 4
    basis = dot(gathered_ref[...].reshape(pairs * two * share, gathered_ref.shape[3]), inverse_ref[...], (1, 1), HIGHEST)
    for k in range(pairs):
        for j in range(two):
            quarter = 2 * ((low + j) % 2) + k % 2
            order = 2 - 2 * j + (second + j * core + k + 1) % 2
            part = basis[(k * two + j) * share : (k * two + j + 1) * share, :]
            at = k // 2 * share
            basis_ref[pl.ds(pl.multiple_of(quarter * rows + at, share), share), :] = part
            half_ref[pl.ds(pl.multiple_of(order * rows + at, share), share), :] = part.astype(BF16)
    coeffs = dot(half_ref[...], tile_ref[...], (0, 0))
    scale = 1.0 / jnp.sqrt(jnp.full((1, 1), total_of(where_ref), F32))
    coeff_ref[...] = (coeffs * scale).reshape(coeff_ref.shape)
    for i in range(keep_ref.shape[0]):
        keep_ref[i] = coeff_ref[2 * i + core]
        send_ref[i] = coeff_ref[2 * i + 1 - core]


def light_pairs(count, reach):
    pairs = []
    for core in range(2):
        shift = core * reach
        for z in range(count):
            pairs.append((core * count + z, core * count + ((((z - shift) % count) ^ reach) + shift) % count))
    return pairs


def across(value, reach):
    return lax.ppermute(value, ("core", *LIGHT), light_pairs(lax.axis_size(LIGHT), reach))


def across_cores(value):
    return lax.ppermute(value, "core", [(0, 1), (1, 0)])


def each_to_each(parts, axes):
    return lax.all_to_all(parts, axes, 0, 0, tiled=True)


def to_each(value, axes):
    return each_to_each(jnp.broadcast_to(value, (lax.axis_size(axes), *value.shape)), axes)


def on_device(tex_feat, light_feat, sketch, row_counts):
    capacity, width = tex_feat.shape[0], sketch.shape[1]
    lights = light_feat.shape[0]
    texels, places = lax.axis_size(TEXEL), lax.axis_size(LIGHT)
    share_rows = capacity // places
    marks = [lax.axis_index(axes) for axes in (TEXEL, "z0", "z1", "core")]
    where = jnp.concatenate([jnp.stack(marks).astype(jnp.int32), row_counts])

    inputs = (where, tex_feat, light_feat, sketch)
    tiles, part = tile_call(0, *inputs)
    passing = across(part, 1)
    tiles, part = tile_call(1, *inputs, tiles)
    staying = across(part, 1)
    tiles, part = tile_call(2, *inputs, tiles)
    passed = across(part + passing, 2)
    tiles, part = tile_call(3, *inputs, tiles)
    quarter = part + staying + passed
    share = jnp.sum(each_to_each(quarter.reshape(places // 4, share_rows, width), FAR), axis=0)

    both = jnp.stack([share, lax.ppermute(share, "z0", [(0, 1), (1, 0)])])
    gram = on_core(gram_kernel, jax.ShapeDtypeStruct((width, width), F32), [VMEM], "gram_part")(share)
    gram, both = lax.optimization_barrier((gram, both))
    gathered = lax.all_gather(both, FAR + ("z1",), axis=0)
    gram_rows = jnp.sum(each_to_each(gram.reshape(texels, width // texels, width), TEXEL), axis=0)
    gram_rows = jnp.sum(to_each(gram_rows, LIGHT), axis=0)
    gram = to_each(gram_rows, TEXEL).reshape(width, width)
    inverse = on_core(
        inverse_kernel,
        jax.ShapeDtypeStruct((width, width), F32),
        [SMEM, VMEM],
        "inverse_factor",
        [pltpu.VMEM((width, width), F32)] * 2,
        10**10,
    )(where, gram)

    lines, chips = width // texels, lax.axis_size(CHIP)
    basis, keep, send = on_core(
        basis_kernel,
        (
            jax.ShapeDtypeStruct((capacity, width), F32),
            jax.ShapeDtypeStruct((chips, lines, lights), F32),
            jax.ShapeDtypeStruct((chips, lines, lights), F32),
        ),
        [SMEM] + [VMEM] * 3,
        "basis_and_coeffs",
        [pltpu.VMEM((capacity, width), BF16), pltpu.VMEM((texels, lines, lights), F32)],
    )(where, inverse, gathered, tiles)
    mine = keep + across_cores(send)
    coeffs = jnp.sum(each_to_each(mine, CHIP), axis=0)
    return basis, coeffs


def solution(mesh):
    fine = Mesh(np.asarray(mesh.devices).reshape(4, 4, 2, 2, 2, 2, 2), (*TEXEL, *LIGHT))
    placed = (P(TEXEL, None), P(LIGHT, None), P(LIGHT, None), P())
    return jax.shard_map(
        on_device, mesh=fine, in_specs=placed, out_specs=(P(TEXEL, None), P(TEXEL, LIGHT)), check_vma=False
    )
```

```python
import math

import jax
import jax.numpy as jnp
import numpy as np
from jax import lax
from jax.experimental import pallas as pl
from jax.experimental.pallas import tpu as pltpu
from jax.sharding import Mesh, PartitionSpec as P

F32 = jnp.float32
BF16 = jnp.bfloat16
CHIP = ("x", "y")
TEXEL = CHIP + ("core",)
FAR = ("z3", "z2")
LIGHT = FAR + ("z1", "z0")
HIGHEST = lax.Precision.HIGHEST
VMEM_LIMIT = 24 * 2**20
COUNTS = 4


def sine_coefficients():
    angle = (np.arange(4000) + 0.5) * math.pi / 4000
    u = 0.125 * (1 + np.cos(angle)) + 1e-9
    w = 1.0
    basis = np.stack([u ** (2 * i + 1) for i in range(5)], axis=1)
    fit, *_ = np.linalg.lstsq(basis / w, np.sin(2 * math.pi * u) / w, rcond=None)
    return [float(c) for c in fit]


SINE = sine_coefficients()
ROUNDER = float(1.5 * 2**23)


def sine(x):
    turns = x * F32(1 / (2 * math.pi))
    part = turns - ((turns + F32(ROUNDER)) - F32(ROUNDER))
    part = jnp.maximum(jnp.minimum(part, F32(0.5) - part), F32(-0.5) - part)
    sq = part * part
    value = F32(SINE[4])
    for c in SINE[3::-1]:
        value = value * sq + F32(c)
    return value * part


def dot(a, b, contract, precision=None):
    return lax.dot_general(
        a, b, ((contract[0:1], contract[1:2]), ((), ())), precision=precision, preferred_element_type=F32
    )


VMEM = pl.BlockSpec(memory_space=pltpu.VMEM)
SMEM = pl.BlockSpec(memory_space=pltpu.SMEM)


def on_core(kernel, out_shape, in_specs, name, scratch=(), flops=10**9, aliases=None):
    return pl.pallas_call(
        kernel,
        out_shape=out_shape,
        in_specs=in_specs,
        out_specs=jax.tree.map(lambda _: VMEM, out_shape),
        scratch_shapes=scratch,
        input_output_aliases=aliases or {},
        compiler_params=pltpu.CompilerParams(vmem_limit_bytes=VMEM_LIMIT),
        cost_estimate=pl.CostEstimate(flops=flops, bytes_accessed=2**20, transcendentals=0),
        name=name,
    )


def quarter_of(order, where):
    low, second, core = where[1], where[2], where[3]
    if order < 2:
        return 2 * (1 - low) + (second + core + 1 - order) % 2
    return 2 * low + (second + 1 - (order - 2)) % 2


def tile_kernel(where_ref, tex_ref, light_ref, sketch_ref, *refs, order, step=128):
    tile_ref, part_ref = refs[-2:]
    rows = part_ref.shape[0]
    first = quarter_of(order, where_ref) * rows
    count = where_ref[COUNTS + where_ref[0]]
    for at in range(0, rows, step):
        tex = tex_ref[pl.ds(pl.multiple_of(first + at, step), step), :]
        tile = sine(dot(tex, light_ref[...], (1, 1))).astype(BF16)
        tile_ref[order * rows + at : order * rows + at + step, :] = tile
        part = dot(tile, sketch_ref[...], (1, 0))
        row = first + at + lax.broadcasted_iota(jnp.int32, part.shape, 0)
        part_ref[at : at + step, :] = jnp.where(row < count, part, 0.0)


def tile_call(order, where, tex, light, sketch, *tiles):
    rows, lights, width = tex.shape[0] // 4, light.shape[0], sketch.shape[1]
    return on_core(
        lambda *refs: tile_kernel(*refs, order=order),
        (jax.ShapeDtypeStruct((tex.shape[0], lights), BF16), jax.ShapeDtypeStruct((rows, width), F32)),
        [SMEM] + [VMEM] * (3 + len(tiles)),
        "tile_quarter",
        flops=2 * rows * lights * (tex.shape[1] + width),
        aliases={4: 0} if tiles else None,
    )(where, tex, light, sketch, *tiles)


def gram_kernel(rows_ref, gram_ref):
    rows = rows_ref[...].reshape(-1, rows_ref.shape[-1])
    gram_ref[...] = dot(rows, rows, (0, 0), HIGHEST)


def invert_factor(gram, y_ref, a_ref, w_ref):
    size = gram.shape[0]
    row = lax.broadcasted_iota(jnp.int32, (size, size), 0)
    col = lax.broadcasted_iota(jnp.int32, (size, size), 1)
    diagonal = jnp.sum(jnp.where(row == col, gram, 0.0), axis=0, keepdims=True)
    a_ref[...] = gram
    y_ref[...] = jnp.where(row == col, lax.rsqrt(diagonal), 0.0)

    def refine(exact):
        precision = HIGHEST if exact else None
        cast = (lambda v: v) if exact else (lambda v: v.astype(BF16))
        y = cast(y_ref[...])
        product = dot(dot(y, cast(a_ref[...]), (1, 0), precision).astype(y.dtype), y, (1, 1), precision)
        off = product - jnp.where(row == col, F32(1), F32(0))
        step = jnp.where(row > col, off, jnp.where(row == col, 0.5 * off, 0.0))
        y_ref[...] = y_ref[...] - dot(cast(step), y, (1, 0), precision)
        return jnp.sum(off * off)

    def coarse(state):
        count, _ = state
        return count + 1, refine(False)

    def fine(state):
        count, _ = state
        return count + 1, refine(True)

    lax.while_loop(lambda s: (s[0] < 8) & (s[1] > 2e-2), coarse, (jnp.int32(0), F32(1)))
    _, rest = lax.while_loop(lambda s: (s[0] < 8) & (s[1] > 4e-6), fine, (jnp.int32(0), F32(1)))

    @pl.when(jnp.logical_not(rest <= 4e-6))
    def _():
        y_ref[...] = jnp.where(row == col, F32(1), F32(0))
        line = lax.broadcasted_iota(jnp.int32, (size, 1), 0)
        w_ref[...] = gram

        def eliminate(j, carry):
            work = w_ref[...]
            column = jnp.sum(jnp.where(col == j, work, 0.0), axis=1, keepdims=True)
            pivot = lax.rsqrt(jnp.sum(jnp.where(line == j, column, 0.0), axis=0, keepdims=True))
            top = w_ref[pl.ds(j, 1), :] * pivot
            top_y = y_ref[pl.ds(j, 1), :] * pivot
            factor = jnp.where(line > j, column * pivot, 0.0)
            w_ref[...] = work - factor * top
            y_ref[...] = jnp.where(line == j, top_y, y_ref[...] - factor * top_y)
            return carry

        lax.fori_loop(0, size, eliminate, 0)


def total_of(where_ref):
    total = F32(0)
    for i in range(COUNTS, where_ref.shape[0]):
        total = total + where_ref[i].astype(F32)
    return total


def basis_kernel(
    where_ref, gram_ref, own_ref, other_ref, tile_ref,
    basis_ref, keep_ref, send_ref, inverse_ref, a_ref, w_ref, half_ref, coeff_ref,
):
    total = total_of(where_ref)
    invert_factor(gram_ref[...] / total, inverse_ref, a_ref, w_ref)
    owners, share = own_ref.shape[:2]
    low, second, core = where_ref[1], where_ref[2], where_ref[3]
    rows = basis_ref.shape[0] // 4
    for j, ref in enumerate((own_ref, other_ref)):
        basis = dot(ref[...].reshape(owners * share, ref.shape[2]), inverse_ref[...], (1, 1), HIGHEST)
        for k in range(owners):
            quarter = 2 * ((low + j) % 2) + k % 2
            order = 2 - 2 * j + (second + j * core + k + 1) % 2
            part = basis[k * share : (k + 1) * share, :]
            at = k // 2 * share
            basis_ref[pl.ds(pl.multiple_of(quarter * rows + at, share), share), :] = part
            half_ref[pl.ds(pl.multiple_of(order * rows + at, share), share), :] = part.astype(BF16)
    coeffs = dot(half_ref[...], tile_ref[...], (0, 0))
    scale = 1.0 / jnp.sqrt(jnp.full((1, 1), total, F32))
    coeff_ref[...] = (coeffs * scale).reshape(coeff_ref.shape)
    for i in range(keep_ref.shape[0]):
        keep_ref[i] = coeff_ref[2 * i + core]
        send_ref[i] = coeff_ref[2 * i + 1 - core]


def light_pairs(count, reach):
    pairs = []
    for core in range(2):
        shift = core * reach
        for z in range(count):
            pairs.append((core * count + z, core * count + ((((z - shift) % count) ^ reach) + shift) % count))
    return pairs


def across(value, reach):
    return lax.ppermute(value, ("core", *LIGHT), light_pairs(lax.axis_size(LIGHT), reach))


def across_cores(value):
    return lax.ppermute(value, "core", [(0, 1), (1, 0)])


def each_to_each(parts, axes):
    return lax.all_to_all(parts, axes, 0, 0, tiled=True)


def to_each(value, axes):
    return each_to_each(jnp.broadcast_to(value, (lax.axis_size(axes), *value.shape)), axes)


def on_device(tex_feat, light_feat, sketch, row_counts):
    capacity, width = tex_feat.shape[0], sketch.shape[1]
    lights = light_feat.shape[0]
    texels, places = lax.axis_size(TEXEL), lax.axis_size(LIGHT)
    share_rows = capacity // places
    marks = [lax.axis_index(axes) for axes in (TEXEL, "z0", "z1", "core")]
    where = jnp.concatenate([jnp.stack(marks).astype(jnp.int32), row_counts])

    inputs = (where, tex_feat, light_feat, sketch)
    tiles, part = tile_call(0, *inputs)
    passing = across(part, 1)
    tiles, turned = tile_call(2, *inputs, tiles)
    tiles, part = tile_call(1, *inputs, tiles)
    staying = across(part, 1)
    passed = across(turned + passing, 2)
    tiles, part = tile_call(3, *inputs, tiles)
    quarter = part + staying + passed
    share = jnp.sum(each_to_each(quarter.reshape(places // 4, share_rows, width), FAR), axis=0)

    own = lax.all_gather(share, FAR + ("z1",), axis=0)
    gram = on_core(gram_kernel, jax.ShapeDtypeStruct((width, width), F32), [VMEM], "gram_part")(own)
    other = across(own, 1)
    gram_rows = jnp.sum(each_to_each(gram.reshape(texels, width // texels, width), TEXEL), axis=0)
    gram_rows, other = lax.optimization_barrier((gram_rows, other))
    gram_rows = gram_rows + lax.ppermute(gram_rows, "z0", [(0, 1), (1, 0)])
    gram = to_each(gram_rows, TEXEL).reshape(width, width)

    lines, chips = width // texels, lax.axis_size(CHIP)
    basis, keep, send = on_core(
        basis_kernel,
        (
            jax.ShapeDtypeStruct((capacity, width), F32),
            jax.ShapeDtypeStruct((chips, lines, lights), F32),
            jax.ShapeDtypeStruct((chips, lines, lights), F32),
        ),
        [SMEM] + [VMEM] * 4,
        "basis_and_coeffs",
        [pltpu.VMEM((width, width), F32)] * 3
        + [pltpu.VMEM((capacity, width), BF16), pltpu.VMEM((texels, lines, lights), F32)],
    )(where, gram, own, other, tiles)
    mine = keep + across_cores(send)
    coeffs = jnp.sum(each_to_each(mine, CHIP), axis=0)
    return basis, coeffs


def solution(mesh):
    fine = Mesh(np.asarray(mesh.devices).reshape(4, 4, 2, 2, 2, 2, 2), (*TEXEL, *LIGHT))
    placed = (P(TEXEL, None), P(LIGHT, None), P(LIGHT, None), P())
    return jax.shard_map(
        on_device, mesh=fine, in_specs=placed, out_specs=(P(TEXEL, None), P(TEXEL, LIGHT)), check_vma=False
    )
```

```python
import functools
import math

import jax
import jax.numpy as jnp
import numpy as np
from jax import lax
from jax.experimental import pallas as pl
from jax.experimental.pallas import tpu as pltpu
from jax.sharding import Mesh, PartitionSpec as P

F32 = jnp.float32
BF16 = jnp.bfloat16
CHIP = ("x", "y")
TEXEL = CHIP + ("core",)
FAR = ("z3", "z2")
LIGHT = FAR + ("z1", "z0")
HIGHEST = lax.Precision.HIGHEST
VMEM_LIMIT = 24 * 2**20


def sine_coefficients():
    angle = (np.arange(4000) + 0.5) * math.pi / 4000
    u = 0.125 * (1 + np.cos(angle)) + 1e-9
    w = 1.0
    basis = np.stack([u ** (2 * i + 1) for i in range(5)], axis=1)
    fit, *_ = np.linalg.lstsq(basis / w, np.sin(2 * math.pi * u) / w, rcond=None)
    return [float(c) for c in fit]


SINE = sine_coefficients()
ROUNDER = float(1.5 * 2**23)


def sine(x):
    turns = x * F32(1 / (2 * math.pi))
    part = turns - ((turns + F32(ROUNDER)) - F32(ROUNDER))
    part = jnp.maximum(jnp.minimum(part, F32(0.5) - part), F32(-0.5) - part)
    sq = part * part
    value = F32(SINE[4])
    for c in SINE[3::-1]:
        value = value * sq + F32(c)
    return value * part


def dot(a, b, contract, precision=None):
    return lax.dot_general(
        a, b, ((contract[0:1], contract[1:2]), ((), ())), precision=precision, preferred_element_type=F32
    )


VMEM = pl.BlockSpec(memory_space=pltpu.VMEM)


def on_core(kernel, out_shape, name, scratch=(), flops=10**9, aliases=None):
    call = lambda *operands: pl.pallas_call(
        kernel,
        out_shape=out_shape,
        in_specs=[VMEM] * len(operands),
        out_specs=jax.tree.map(lambda _: VMEM, out_shape),
        scratch_shapes=scratch,
        input_output_aliases=aliases or {},
        compiler_params=pltpu.CompilerParams(vmem_limit_bytes=VMEM_LIMIT),
        cost_estimate=pl.CostEstimate(flops=flops, bytes_accessed=2**20, transcendentals=0),
        name=name,
    )(*operands)
    return call


def quarter_of(order):
    low, second, core = (lax.axis_index(axis) for axis in ("z0", "z1", "core"))
    if order < 2:
        return 2 * (1 - low) + (second + core + 1 - order) % 2
    return 2 * low + (second + 1 - (order - 2)) % 2


def tile_kernel(tex_ref, light_ref, sketch_ref, *refs, order, step=128):
    tile_ref, part_ref = refs[-2:]
    rows = part_ref.shape[0]
    first = quarter_of(order) * rows
    for at in range(0, rows, step):
        tex = tex_ref[pl.ds(pl.multiple_of(first + at, step), step), :]
        tile = sine(dot(tex, light_ref[...], (1, 1))).astype(BF16)
        tile_ref[order * rows + at : order * rows + at + step, :] = tile
        part_ref[at : at + step, :] = dot(tile, sketch_ref[...], (1, 0))


def tile_call(order, tex, light, sketch, *tiles):
    rows, lights, width = tex.shape[0] // 4, light.shape[0], sketch.shape[1]
    return on_core(
        functools.partial(tile_kernel, order=order),
        (jax.ShapeDtypeStruct((tex.shape[0], lights), BF16), jax.ShapeDtypeStruct((rows, width), F32)),
        "tile_quarter",
        flops=2 * rows * lights * (tex.shape[1] + width),
        aliases={3: 0} if tiles else None,
    )(tex, light, sketch, *tiles)


def gram_kernel(rows_ref, gram_ref):
    gram_ref[...] = dot(rows_ref[...], rows_ref[...], (0, 0), HIGHEST)


def invert_factor(gram, y_ref, a_ref, w_ref):
    size = gram.shape[0]
    row = lax.broadcasted_iota(jnp.int32, (size, size), 0)
    col = lax.broadcasted_iota(jnp.int32, (size, size), 1)
    diagonal = jnp.sum(jnp.where(row == col, gram, 0.0), axis=0, keepdims=True)
    a_ref[...] = gram
    y_ref[...] = jnp.where(row == col, lax.rsqrt(diagonal), 0.0)

    def refine(exact):
        precision = HIGHEST if exact else None
        cast = (lambda v: v) if exact else (lambda v: v.astype(BF16))
        y = cast(y_ref[...])
        product = dot(dot(y, cast(a_ref[...]), (1, 0), precision).astype(y.dtype), y, (1, 1), precision)
        off = product - jnp.where(row == col, F32(1), F32(0))
        step = jnp.where(row > col, off, jnp.where(row == col, 0.5 * off, 0.0))
        y_ref[...] = y_ref[...] - dot(cast(step), y, (1, 0), precision)
        return jnp.sum(off * off)

    def coarse(state):
        count, _ = state
        return count + 1, refine(False)

    def fine(state):
        count, _ = state
        return count + 1, refine(True)

    lax.while_loop(lambda s: (s[0] < 8) & (s[1] > 2e-2), coarse, (jnp.int32(0), F32(1)))
    _, rest = lax.while_loop(lambda s: (s[0] < 8) & (s[1] > 4e-6), fine, (jnp.int32(0), F32(1)))

    @pl.when(jnp.logical_not(rest <= 4e-6))
    def _():
        y_ref[...] = jnp.where(row == col, F32(1), F32(0))
        line = lax.broadcasted_iota(jnp.int32, (size, 1), 0)
        w_ref[...] = gram

        def eliminate(j, carry):
            work = w_ref[...]
            column = jnp.sum(jnp.where(col == j, work, 0.0), axis=1, keepdims=True)
            pivot = lax.rsqrt(jnp.sum(jnp.where(line == j, column, 0.0), axis=0, keepdims=True))
            top = w_ref[pl.ds(j, 1), :] * pivot
            top_y = y_ref[pl.ds(j, 1), :] * pivot
            factor = jnp.where(line > j, column * pivot, 0.0)
            w_ref[...] = work - factor * top
            y_ref[...] = jnp.where(line == j, top_y, y_ref[...] - factor * top_y)
            return carry

        lax.fori_loop(0, size, eliminate, 0)


def basis_kernel(
    total_ref, gram_ref, own_ref, other_ref, tile_ref,
    basis_ref, keep_ref, send_ref, inverse_ref, a_ref, w_ref, half_ref, coeff_ref,
):
    total = total_ref[...]
    invert_factor(gram_ref[...] / total, inverse_ref, a_ref, w_ref)
    rows = basis_ref.shape[0] // 4
    for ref, orders in ((own_ref, (3, 2)), (other_ref, (1, 0))):
        basis = dot(ref[...], inverse_ref[...], (1, 1), HIGHEST)
        for i, order in enumerate(orders):
            part = basis[i * rows : (i + 1) * rows, :]
            basis_ref[pl.ds(pl.multiple_of(quarter_of(order) * rows, rows), rows), :] = part
            half_ref[order * rows : (order + 1) * rows, :] = part.astype(BF16)
    coeffs = dot(half_ref[...], tile_ref[...], (0, 0))
    coeff_ref[...] = (coeffs * (1.0 / jnp.sqrt(total))).reshape(coeff_ref.shape)
    core = lax.axis_index("core")
    for i in range(keep_ref.shape[0]):
        keep_ref[i] = coeff_ref[2 * i + core]
        send_ref[i] = coeff_ref[2 * i + 1 - core]


def light_pairs(count, reach):
    pairs = []
    for core in range(2):
        shift = core * reach
        for z in range(count):
            pairs.append((core * count + z, core * count + ((((z - shift) % count) ^ reach) + shift) % count))
    return pairs


def across(value, reach):
    return lax.ppermute(value, ("core", *LIGHT), light_pairs(lax.axis_size(LIGHT), reach))


def across_cores(value):
    return lax.ppermute(value, "core", [(0, 1), (1, 0)])


def each_to_each(parts, axes):
    return lax.all_to_all(parts, axes, 0, 0, tiled=True)


def to_each(value, axes):
    return each_to_each(jnp.broadcast_to(value, (lax.axis_size(axes), *value.shape)), axes)


def on_device(tex_feat, light_feat, sketch, row_counts):
    capacity, width = tex_feat.shape[0], sketch.shape[1]
    lights = light_feat.shape[0]
    texels, places = lax.axis_size(TEXEL), lax.axis_size(LIGHT)
    share_rows = capacity // places
    total = jnp.sum(row_counts).astype(F32).reshape(1, 1)
    used = row_counts[lax.axis_index(TEXEL)] - quarter_of(3) * (capacity // 4) - lax.axis_index(FAR) * share_rows

    inputs = (tex_feat, light_feat, sketch)
    tiles, part = tile_call(0, *inputs)
    passing = across(part, 1)
    tiles, part = tile_call(2, *inputs, tiles)
    tiles, passing = lax.optimization_barrier((tiles, passing))
    passed = across(part + passing, 2)
    tiles, part = tile_call(1, *inputs, tiles)
    staying = across(part, 1)
    tiles, part = tile_call(3, *inputs, tiles)
    quarter = part + staying + passed
    share = jnp.sum(each_to_each(quarter.reshape(places // 4, share_rows, width), FAR), axis=0)
    share = jnp.where(lax.broadcasted_iota(jnp.int32, share.shape, 0) < used, share, 0.0)

    quarter = lax.all_gather(share, FAR, axis=0, tiled=True)
    near = across(quarter, 2)
    gram = on_core(gram_kernel, jax.ShapeDtypeStruct((width, width), F32), "gram_part")(quarter)
    gram_rows = jnp.sum(each_to_each(gram.reshape(texels, width // texels, width), TEXEL), axis=0)
    gram_rows, near = lax.optimization_barrier((gram_rows, near))
    own = jnp.concatenate([quarter, near])
    other = across(own, 1)
    gram_rows = jnp.sum(to_each(gram_rows, ("z1", "z0")), axis=0)
    gram = to_each(gram_rows, TEXEL).reshape(width, width)

    lines, chips = width // texels, lax.axis_size(CHIP)
    basis, keep, send = on_core(
        basis_kernel,
        (
            jax.ShapeDtypeStruct((capacity, width), F32),
            jax.ShapeDtypeStruct((chips, lines, lights), F32),
            jax.ShapeDtypeStruct((chips, lines, lights), F32),
        ),
        "basis_and_coeffs",
        [pltpu.VMEM((width, width), F32)] * 3
        + [pltpu.VMEM((capacity, width), BF16), pltpu.VMEM((texels, lines, lights), F32)],
    )(total, gram, own, other, tiles)
    mine = keep + across_cores(send)
    coeffs = jnp.sum(each_to_each(mine, CHIP), axis=0)
    return basis, coeffs


def solution(mesh):
    fine = Mesh(np.asarray(mesh.devices).reshape(4, 4, 2, 2, 2, 2, 2), (*TEXEL, *LIGHT))
    placed = (P(TEXEL, None), P(LIGHT, None), P(LIGHT, None), P())
    return jax.shard_map(
        on_device, mesh=fine, in_specs=placed, out_specs=(P(TEXEL, None), P(TEXEL, LIGHT)), check_vma=False
    )
```

```python
import functools
import math

import jax
import jax.numpy as jnp
import numpy as np
from jax import lax
from jax.experimental import pallas as pl
from jax.experimental.pallas import tpu as pltpu
from jax.sharding import Mesh, PartitionSpec as P

F32 = jnp.float32
BF16 = jnp.bfloat16
CHIP = ("x", "y")
TEXEL = CHIP + ("core",)
FAR = ("z3", "z2")
LIGHT = FAR + ("z1", "z0")
HIGHEST = lax.Precision.HIGHEST
VMEM_LIMIT = 24 * 2**20


def sine_coefficients():
    angle = (np.arange(4000) + 0.5) * math.pi / 4000
    u = 0.125 * (1 + np.cos(angle)) + 1e-9
    w = 1.0
    basis = np.stack([u ** (2 * i + 1) for i in range(5)], axis=1)
    fit, *_ = np.linalg.lstsq(basis / w, np.sin(2 * math.pi * u) / w, rcond=None)
    return [float(c) for c in fit]


SINE = sine_coefficients()
ROUNDER = float(1.5 * 2**23)


def sine(x):
    turns = x * F32(1 / (2 * math.pi))
    part = turns - ((turns + F32(ROUNDER)) - F32(ROUNDER))
    part = jnp.maximum(jnp.minimum(part, F32(0.5) - part), F32(-0.5) - part)
    sq = part * part
    value = F32(SINE[4])
    for c in SINE[3::-1]:
        value = value * sq + F32(c)
    return value * part


def dot(a, b, contract, precision=None):
    return lax.dot_general(
        a, b, ((contract[0:1], contract[1:2]), ((), ())), precision=precision, preferred_element_type=F32
    )


VMEM = pl.BlockSpec(memory_space=pltpu.VMEM)


def on_core(kernel, out_shape, name, scratch=(), flops=10**9, aliases=None):
    call = lambda *operands: pl.pallas_call(
        kernel,
        out_shape=out_shape,
        in_specs=[VMEM] * len(operands),
        out_specs=jax.tree.map(lambda _: VMEM, out_shape),
        scratch_shapes=scratch,
        input_output_aliases=aliases or {},
        compiler_params=pltpu.CompilerParams(vmem_limit_bytes=VMEM_LIMIT),
        cost_estimate=pl.CostEstimate(flops=flops, bytes_accessed=2**20, transcendentals=0),
        name=name,
    )(*operands)
    return call


def quarter_of(order):
    low, second, core = (lax.axis_index(axis) for axis in ("z0", "z1", "core"))
    if order < 2:
        return 2 * (1 - low) + (second + core + 1 - order) % 2
    return 2 * low + (second + 1 - (order - 2)) % 2


def split(value):
    high = value.astype(BF16)
    return high, (value - high.astype(F32)).astype(BF16)


def dot_split(a, b, contract):
    (a_high, a_low), (b_high, b_low) = a, b
    return dot(a_high, b_high, contract) + (dot(a_high, b_low, contract) + dot(a_low, b_high, contract))


def tile_kernel(tex_ref, light_ref, sketch_ref, *refs, order, step=128):
    tile_ref, part_ref = refs[-2:]
    rows = part_ref.shape[0]
    first = quarter_of(order) * rows
    for at in range(0, rows, step):
        tex = tex_ref[pl.ds(pl.multiple_of(first + at, step), step), :]
        tile = sine(dot(tex, light_ref[...], (1, 1))).astype(BF16)
        tile_ref[order * rows + at : order * rows + at + step, :] = tile
        part_ref[at : at + step, :] = dot(tile, sketch_ref[...], (1, 0))


def tile_call(order, tex, light, sketch, *tiles):
    rows, lights, width = tex.shape[0] // 4, light.shape[0], sketch.shape[1]
    return on_core(
        functools.partial(tile_kernel, order=order),
        (jax.ShapeDtypeStruct((tex.shape[0], lights), BF16), jax.ShapeDtypeStruct((rows, width), F32)),
        "tile_quarter",
        flops=2 * rows * lights * (tex.shape[1] + width),
        aliases={3: 0} if tiles else None,
    )(tex, light, sketch, *tiles)


def gram_kernel(counts_ref, quarter_ref, near_ref, rows_ref, gram_ref):
    rows = quarter_ref.shape[0]
    texel = lax.broadcasted_iota(jnp.int32, counts_ref.shape, 1)
    count = jnp.sum(jnp.where(texel == lax.axis_index(TEXEL), counts_ref[...], 0), axis=1, keepdims=True)
    row = lax.broadcasted_iota(jnp.int32, quarter_ref.shape, 0)
    rows_ref[:rows, :] = jnp.where(row + quarter_of(3) * rows < count, quarter_ref[...], 0.0)
    rows_ref[rows:, :] = jnp.where(row + quarter_of(2) * rows < count, near_ref[...], 0.0)
    parts = split(rows_ref[...])
    gram_ref[...] = dot_split(parts, parts, (0, 0))


def invert_factor(gram, y_ref, a_ref, w_ref):
    size = gram.shape[0]
    row = lax.broadcasted_iota(jnp.int32, (size, size), 0)
    col = lax.broadcasted_iota(jnp.int32, (size, size), 1)
    diagonal = jnp.sum(jnp.where(row == col, gram, 0.0), axis=0, keepdims=True)
    a_ref[...] = gram
    y_ref[...] = jnp.where(row == col, lax.rsqrt(diagonal), 0.0)

    def refine(exact):
        precision = HIGHEST if exact else None
        cast = (lambda v: v) if exact else (lambda v: v.astype(BF16))
        y = cast(y_ref[...])
        product = dot(dot(y, cast(a_ref[...]), (1, 0), precision).astype(y.dtype), y, (1, 1), precision)
        off = product - jnp.where(row == col, F32(1), F32(0))
        step = jnp.where(row > col, off, jnp.where(row == col, 0.5 * off, 0.0))
        y_ref[...] = y_ref[...] - dot(cast(step), y, (1, 0), precision)
        return jnp.sum(off * off)

    def coarse(state):
        count, _ = state
        return count + 1, refine(False)

    def fine(state):
        count, _ = state
        return count + 1, refine(True)

    lax.while_loop(lambda s: (s[0] < 8) & (s[1] > 2e-2), coarse, (jnp.int32(0), F32(1)))
    _, rest = lax.while_loop(lambda s: (s[0] < 8) & (s[1] > 4e-6), fine, (jnp.int32(0), F32(1)))

    @pl.when(jnp.logical_not(rest <= 4e-6))
    def _():
        y_ref[...] = jnp.where(row == col, F32(1), F32(0))
        line = lax.broadcasted_iota(jnp.int32, (size, 1), 0)
        w_ref[...] = gram

        def eliminate(j, carry):
            work = w_ref[...]
            column = jnp.sum(jnp.where(col == j, work, 0.0), axis=1, keepdims=True)
            pivot = lax.rsqrt(jnp.sum(jnp.where(line == j, column, 0.0), axis=0, keepdims=True))
            top = w_ref[pl.ds(j, 1), :] * pivot
            top_y = y_ref[pl.ds(j, 1), :] * pivot
            factor = jnp.where(line > j, column * pivot, 0.0)
            w_ref[...] = work - factor * top
            y_ref[...] = jnp.where(line == j, top_y, y_ref[...] - factor * top_y)
            return carry

        lax.fori_loop(0, size, eliminate, 0)


def basis_kernel(
    total_ref, gram_ref, own_ref, other_ref, tile_ref,
    basis_ref, keep_ref, send_ref, inverse_ref, a_ref, w_ref, half_ref, coeff_ref,
):
    total = total_ref[...]
    invert_factor(gram_ref[...] / total, inverse_ref, a_ref, w_ref)
    rows = basis_ref.shape[0] // 4
    inverse = split(inverse_ref[...])
    for ref, orders in ((own_ref, (3, 2)), (other_ref, (1, 0))):
        basis = dot_split(split(ref[...]), inverse, (1, 1))
        for i, order in enumerate(orders):
            part = basis[i * rows : (i + 1) * rows, :]
            basis_ref[pl.ds(pl.multiple_of(quarter_of(order) * rows, rows), rows), :] = part
            half_ref[order * rows : (order + 1) * rows, :] = part.astype(BF16)
    coeffs = dot(half_ref[...], tile_ref[...], (0, 0))
    coeff_ref[...] = (coeffs * (1.0 / jnp.sqrt(total))).reshape(coeff_ref.shape)
    core = lax.axis_index("core")
    for i in range(keep_ref.shape[0]):
        keep_ref[i] = coeff_ref[2 * i + core]
        send_ref[i] = coeff_ref[2 * i + 1 - core]


def light_pairs(count, reach):
    pairs = []
    for core in range(2):
        shift = core * reach
        for z in range(count):
            pairs.append((core * count + z, core * count + ((((z - shift) % count) ^ reach) + shift) % count))
    return pairs


def across(value, reach):
    return lax.ppermute(value, ("core", *LIGHT), light_pairs(lax.axis_size(LIGHT), reach))


def across_cores(value):
    return lax.ppermute(value, "core", [(0, 1), (1, 0)])


def each_to_each(parts, axes):
    return lax.all_to_all(parts, axes, 0, 0, tiled=True)


def to_each(value, axes):
    return each_to_each(jnp.broadcast_to(value, (lax.axis_size(axes), *value.shape)), axes)


def on_device(tex_feat, light_feat, sketch, row_counts):
    capacity, width = tex_feat.shape[0], sketch.shape[1]
    lights = light_feat.shape[0]
    texels, places = lax.axis_size(TEXEL), lax.axis_size(LIGHT)
    share_rows = capacity // places
    total = jnp.sum(row_counts).astype(F32).reshape(1, 1)

    inputs = (tex_feat, light_feat, sketch)
    tiles, part = tile_call(0, *inputs)
    passing = across(part, 1)
    tiles, turned = tile_call(2, *inputs, tiles)
    tiles, part = tile_call(1, *inputs, tiles)
    staying = across(part, 1)
    passed = across(turned + passing, 2)
    tiles, part = tile_call(3, *inputs, tiles)
    quarter = part + staying + passed
    share = jnp.sum(each_to_each(quarter.reshape(places // 4, share_rows, width), FAR), axis=0)

    quarter = lax.all_gather(share, FAR, axis=0, tiled=True)
    half_shape, square = (capacity // 2, width), (width, width)
    own, gram = on_core(
        gram_kernel, (jax.ShapeDtypeStruct(half_shape, F32), jax.ShapeDtypeStruct(square, F32)), "gram_part"
    )(row_counts.reshape(1, texels), quarter, across(quarter, 2))
    other = across(own, 1)
    gram_rows = jnp.sum(each_to_each(gram.reshape(texels, width // texels, width), TEXEL), axis=0)
    gram_rows, other = lax.optimization_barrier((gram_rows, other))
    gram_rows = gram_rows + lax.ppermute(gram_rows, "z0", [(0, 1), (1, 0)])
    gram = to_each(gram_rows, TEXEL).reshape(square)

    lines, chips = width // texels, lax.axis_size(CHIP)
    basis, keep, send = on_core(
        basis_kernel,
        (
            jax.ShapeDtypeStruct((capacity, width), F32),
            jax.ShapeDtypeStruct((chips, lines, lights), F32),
            jax.ShapeDtypeStruct((chips, lines, lights), F32),
        ),
        "basis_and_coeffs",
        [pltpu.VMEM(square, F32)] * 3
        + [pltpu.VMEM((capacity, width), BF16), pltpu.VMEM((texels, lines, lights), F32)],
    )(total, gram, own, other, tiles)
    mine = keep + across_cores(send)
    coeffs = jnp.sum(each_to_each(mine, CHIP), axis=0)
    return basis, coeffs


def solution(mesh):
    fine = Mesh(np.asarray(mesh.devices).reshape(4, 4, 2, 2, 2, 2, 2), (*TEXEL, *LIGHT))
    placed = (P(TEXEL, None), P(LIGHT, None), P(LIGHT, None), P())
    return jax.shard_map(
        on_device, mesh=fine, in_specs=placed, out_specs=(P(TEXEL, None), P(TEXEL, LIGHT)), check_vma=False
    )
```

```python
import functools
import math

import jax
import jax.numpy as jnp
import numpy as np
from jax import lax
from jax.experimental import pallas as pl
from jax.experimental.pallas import tpu as pltpu
from jax.sharding import Mesh, PartitionSpec as P

F32 = jnp.float32
BF16 = jnp.bfloat16
CHIP = ("x", "y")
TEXEL = CHIP + ("core",)
FAR = ("z3", "z2")
LIGHT = FAR + ("z1", "z0")
HIGHEST = lax.Precision.HIGHEST
VMEM_LIMIT = 24 * 2**20


def sine_coefficients():
    angle = (np.arange(4000) + 0.5) * math.pi / 4000
    u = 0.125 * (1 + np.cos(angle)) + 1e-9
    w = 1.0
    basis = np.stack([u ** (2 * i + 1) for i in range(5)], axis=1)
    fit, *_ = np.linalg.lstsq(basis / w, np.sin(2 * math.pi * u) / w, rcond=None)
    return [float(c) for c in fit]


SINE = sine_coefficients()
ROUNDER = float(1.5 * 2**23)


def sine(x):
    turns = x * F32(1 / (2 * math.pi))
    part = turns - ((turns + F32(ROUNDER)) - F32(ROUNDER))
    part = jnp.maximum(jnp.minimum(part, F32(0.5) - part), F32(-0.5) - part)
    sq = part * part
    value = F32(SINE[4])
    for c in SINE[3::-1]:
        value = value * sq + F32(c)
    return value * part


def dot(a, b, contract, precision=None):
    return lax.dot_general(
        a, b, ((contract[0:1], contract[1:2]), ((), ())), precision=precision, preferred_element_type=F32
    )


VMEM = pl.BlockSpec(memory_space=pltpu.VMEM)


def on_core(kernel, out_shape, name, scratch=(), flops=10**9, aliases=None):
    call = lambda *operands: pl.pallas_call(
        kernel,
        out_shape=out_shape,
        in_specs=[VMEM] * len(operands),
        out_specs=jax.tree.map(lambda _: VMEM, out_shape),
        scratch_shapes=scratch,
        input_output_aliases=aliases or {},
        compiler_params=pltpu.CompilerParams(vmem_limit_bytes=VMEM_LIMIT),
        cost_estimate=pl.CostEstimate(flops=flops, bytes_accessed=2**20, transcendentals=0),
        name=name,
    )(*operands)
    return call


def quarter_of(order):
    low, second, core = (lax.axis_index(axis) for axis in ("z0", "z1", "core"))
    if order < 2:
        return 2 * (1 - low) + (second + core + 1 - order) % 2
    return 2 * low + (second + 1 - (order - 2)) % 2


def split(value):
    high = value.astype(BF16)
    return high, (value - high.astype(F32)).astype(BF16)


def dot_split(a, b, contract):
    (a_high, a_low), (b_high, b_low) = a, b
    return dot(a_high, b_high, contract) + (dot(a_high, b_low, contract) + dot(a_low, b_high, contract))


def tile_kernel(tex_ref, light_ref, sketch_ref, *refs, order, step=128):
    tile_ref, part_ref = refs[-2:]
    rows = part_ref.shape[0]
    first = quarter_of(order) * rows
    for at in range(0, rows, step):
        tex = tex_ref[pl.ds(pl.multiple_of(first + at, step), step), :]
        tile = sine(dot(tex, light_ref[...], (1, 1))).astype(BF16)
        tile_ref[order * rows + at : order * rows + at + step, :] = tile
        part_ref[at : at + step, :] = dot(tile, sketch_ref[...], (1, 0))


def tile_call(order, tex, light, sketch, *tiles):
    rows, lights, width = tex.shape[0] // 4, light.shape[0], sketch.shape[1]
    return on_core(
        functools.partial(tile_kernel, order=order),
        (jax.ShapeDtypeStruct((tex.shape[0], lights), BF16), jax.ShapeDtypeStruct((rows, width), F32)),
        "tile_quarter",
        flops=2 * rows * lights * (tex.shape[1] + width),
        aliases={3: 0} if tiles else None,
    )(tex, light, sketch, *tiles)


def mask_kernel(counts_ref, quarter_ref, rows_ref):
    rows = quarter_ref.shape[0]
    texel = lax.broadcasted_iota(jnp.int32, counts_ref.shape, 1)
    count = jnp.sum(jnp.where(texel == lax.axis_index(TEXEL), counts_ref[...], 0), axis=1, keepdims=True)
    row = lax.broadcasted_iota(jnp.int32, quarter_ref.shape, 0)
    rows_ref[...] = jnp.where(row + quarter_of(3) * rows < count, quarter_ref[...], 0.0)


def gram_kernel(rows_ref, gram_ref):
    parts = split(rows_ref[...])
    gram_ref[...] = dot_split(parts, parts, (0, 0))


def invert_factor(gram, y_ref, a_ref, w_ref):
    size = gram.shape[0]
    row = lax.broadcasted_iota(jnp.int32, (size, size), 0)
    col = lax.broadcasted_iota(jnp.int32, (size, size), 1)

    def lower_half(rest):
        return jnp.where(row > col, rest, jnp.where(row == col, 0.5 * rest, 0.0))

    diagonal = jnp.where(row == col, gram, 0.0)
    across_columns = lax.rsqrt(jnp.sum(diagonal, axis=0, keepdims=True))
    down_rows = lax.rsqrt(jnp.sum(diagonal, axis=1, keepdims=True))
    unit = jnp.where(row == col, F32(1), F32(0))
    a_ref[...] = gram
    y_ref[...] = (unit - lower_half(gram * down_rows * across_columns - unit)) * across_columns

    def refine(exact):
        y = y_ref[...]
        if exact:
            parts = split(y)
            rest = dot_split(split(dot_split(parts, split(a_ref[...]), (1, 0))), parts, (1, 1)) - unit
            y_ref[...] = y - dot_split(split(lower_half(rest)), parts, (1, 0))
        else:
            rough = y.astype(BF16)
            rest = dot(dot(rough, a_ref[...].astype(BF16), (1, 0)).astype(BF16), rough, (1, 1)) - unit
            y_ref[...] = y - dot(lower_half(rest).astype(BF16), rough, (1, 0))
        return jnp.sum(rest * rest)

    def steps(exact, enough):
        return lax.while_loop(
            lambda state: (state[0] < 8) & (state[1] > enough),
            lambda state: (state[0] + 1, refine(exact)),
            (jnp.int32(0), F32(1)),
        )[1]

    steps(False, 1e-1)
    rest = steps(True, 4e-6)

    @pl.when(jnp.logical_not(rest <= 4e-6))
    def _():
        y_ref[...] = unit
        line = lax.broadcasted_iota(jnp.int32, (size, 1), 0)
        w_ref[...] = gram

        def eliminate(j, carry):
            work = w_ref[...]
            column = jnp.sum(jnp.where(col == j, work, 0.0), axis=1, keepdims=True)
            pivot = lax.rsqrt(jnp.sum(jnp.where(line == j, column, 0.0), axis=0, keepdims=True))
            top = w_ref[pl.ds(j, 1), :] * pivot
            top_y = y_ref[pl.ds(j, 1), :] * pivot
            factor = jnp.where(line > j, column * pivot, 0.0)
            w_ref[...] = work - factor * top
            y_ref[...] = jnp.where(line == j, top_y, y_ref[...] - factor * top_y)
            return carry

        lax.fori_loop(0, size, eliminate, 0)


def basis_kernel(total_ref, gram_ref, *refs):
    quarter_refs, tile_ref = refs[:4], refs[4]
    basis_ref, keep_ref, send_ref, inverse_ref, a_ref, w_ref, half_ref, coeff_ref = refs[5:]
    total = total_ref[...]
    invert_factor(gram_ref[...] / total, inverse_ref, a_ref, w_ref)
    rows = basis_ref.shape[0] // 4
    inverse = split(inverse_ref[...])
    for order, ref in enumerate(quarter_refs):
        basis = dot_split(split(ref[...]), inverse, (1, 1))
        basis_ref[pl.ds(pl.multiple_of(quarter_of(order) * rows, rows), rows), :] = basis
        half_ref[order * rows : (order + 1) * rows, :] = basis.astype(BF16)
    coeffs = dot(half_ref[...], tile_ref[...], (0, 0))
    coeff_ref[...] = (coeffs * (1.0 / jnp.sqrt(total))).reshape(coeff_ref.shape)
    core = lax.axis_index("core")
    for i in range(keep_ref.shape[0]):
        keep_ref[i] = coeff_ref[2 * i + core]
        send_ref[i] = coeff_ref[2 * i + 1 - core]


def light_pairs(count, reach):
    pairs = []
    for core in range(2):
        shift = core * reach
        for z in range(count):
            pairs.append((core * count + z, core * count + ((((z - shift) % count) ^ reach) + shift) % count))
    return pairs


def across(value, reach):
    return lax.ppermute(value, ("core", *LIGHT), light_pairs(lax.axis_size(LIGHT), reach))


def across_cores(value):
    return lax.ppermute(value, "core", [(0, 1), (1, 0)])


def each_to_each(parts, axes):
    return lax.all_to_all(parts, axes, 0, 0, tiled=True)


def to_each(value, axes):
    return each_to_each(jnp.broadcast_to(value, (lax.axis_size(axes), *value.shape)), axes)


def on_device(tex_feat, light_feat, sketch, row_counts):
    capacity, width = tex_feat.shape[0], sketch.shape[1]
    lights = light_feat.shape[0]
    texels, places = lax.axis_size(TEXEL), lax.axis_size(LIGHT)
    share_rows = capacity // places
    total = jnp.sum(row_counts).astype(F32).reshape(1, 1)

    inputs = (tex_feat, light_feat, sketch)
    tiles, part = tile_call(0, *inputs)
    passing = across(part, 1)
    tiles, turned = tile_call(2, *inputs, tiles)
    tiles, part = tile_call(1, *inputs, tiles)
    staying = across(part, 1)
    passed = across(turned + passing, 2)
    tiles, part = tile_call(3, *inputs, tiles)
    quarter = part + staying + passed
    share = jnp.sum(each_to_each(quarter.reshape(places // 4, share_rows, width), FAR), axis=0)

    square = (width, width)
    quarter = lax.all_gather(share, FAR, axis=0, tiled=True)
    quarter = on_core(mask_kernel, jax.ShapeDtypeStruct(quarter.shape, F32), "used_rows")(
        row_counts.reshape(1, texels), quarter
    )
    near, beside = across(quarter, 2), across(quarter, 1)
    gram = on_core(gram_kernel, jax.ShapeDtypeStruct(square, F32), "gram_part")(quarter)
    gram_rows = jnp.sum(each_to_each(gram.reshape(texels, width // texels, width), TEXEL), axis=0)
    gram_rows, near, beside = lax.optimization_barrier((gram_rows, near, beside))
    beyond = across(near, 1)
    gram_rows = jnp.sum(to_each(gram_rows, ("z1", "z0")), axis=0)
    gram = to_each(gram_rows, TEXEL).reshape(square)

    lines, chips = width // texels, lax.axis_size(CHIP)
    basis, keep, send = on_core(
        basis_kernel,
        (
            jax.ShapeDtypeStruct((capacity, width), F32),
            jax.ShapeDtypeStruct((chips, lines, lights), F32),
            jax.ShapeDtypeStruct((chips, lines, lights), F32),
        ),
        "basis_and_coeffs",
        [pltpu.VMEM(square, F32)] * 3
        + [pltpu.VMEM((capacity, width), BF16), pltpu.VMEM((texels, lines, lights), F32)],
    )(total, gram, beyond, beside, near, quarter, tiles)
    mine = keep + across_cores(send)
    coeffs = jnp.sum(each_to_each(mine, CHIP), axis=0)
    return basis, coeffs


def solution(mesh):
    fine = Mesh(np.asarray(mesh.devices).reshape(4, 4, 2, 2, 2, 2, 2), (*TEXEL, *LIGHT))
    placed = (P(TEXEL, None), P(LIGHT, None), P(LIGHT, None), P())
    return jax.shard_map(
        on_device, mesh=fine, in_specs=placed, out_specs=(P(TEXEL, None), P(TEXEL, LIGHT)), check_vma=False
    )
```

```python
import functools
import math

import jax
import jax.numpy as jnp
import numpy as np
from jax import lax
from jax.experimental import pallas as pl
from jax.experimental.pallas import tpu as pltpu
from jax.sharding import Mesh, PartitionSpec as P

F32 = jnp.float32
BF16 = jnp.bfloat16
CHIP = ("x", "y")
TEXEL = CHIP + ("core",)
FAR = ("z3", "z2")
LIGHT = FAR + ("z1", "z0")
HIGHEST = lax.Precision.HIGHEST
VMEM_LIMIT = 24 * 2**20


def sine_coefficients():
    angle = (np.arange(4000) + 0.5) * math.pi / 4000
    u = 0.125 * (1 + np.cos(angle)) + 1e-9
    w = 1.0
    basis = np.stack([u ** (2 * i + 1) for i in range(5)], axis=1)
    fit, *_ = np.linalg.lstsq(basis / w, np.sin(2 * math.pi * u) / w, rcond=None)
    return [float(c) for c in fit]


SINE = sine_coefficients()
ROUNDER = float(1.5 * 2**23)


def sine(x):
    turns = x * F32(1 / (2 * math.pi))
    part = turns - ((turns + F32(ROUNDER)) - F32(ROUNDER))
    part = jnp.maximum(jnp.minimum(part, F32(0.5) - part), F32(-0.5) - part)
    sq = part * part
    value = F32(SINE[4])
    for c in SINE[3::-1]:
        value = value * sq + F32(c)
    return value * part


def dot(a, b, contract, precision=None):
    return lax.dot_general(
        a, b, ((contract[0:1], contract[1:2]), ((), ())), precision=precision, preferred_element_type=F32
    )


VMEM = pl.BlockSpec(memory_space=pltpu.VMEM)


def on_core(kernel, out_shape, name, scratch=(), flops=10**9, aliases=None):
    call = lambda *operands: pl.pallas_call(
        kernel,
        out_shape=out_shape,
        in_specs=[VMEM] * len(operands),
        out_specs=jax.tree.map(lambda _: VMEM, out_shape),
        scratch_shapes=scratch,
        input_output_aliases=aliases or {},
        compiler_params=pltpu.CompilerParams(vmem_limit_bytes=VMEM_LIMIT),
        cost_estimate=pl.CostEstimate(flops=flops, bytes_accessed=2**20, transcendentals=0),
        name=name,
    )(*operands)
    return call


def quarter_of(order):
    low, second, core = (lax.axis_index(axis) for axis in ("z0", "z1", "core"))
    if order < 2:
        return 2 * (1 - low) + (second + core + 1 - order) % 2
    return 2 * low + (second + 1 - (order - 2)) % 2


def partner(place, reach):
    places, shift = lax.axis_size(LIGHT), lax.axis_index("core") * reach
    return (((place - shift + places) % places ^ reach) + shift) % places


def split(value):
    high = value.astype(BF16)
    return high, (value - high.astype(F32)).astype(BF16)


def dot_split(a, b, contract):
    (a_high, a_low), (b_high, b_low) = a, b
    return dot(a_high, b_high, contract) + (dot(a_high, b_low, contract) + dot(a_low, b_high, contract))


def tile_kernel(tex_ref, light_ref, sketch_ref, *refs, order, step=128):
    tile_ref, part_ref = refs[-2:]
    rows, groups = part_ref.shape[0], lax.axis_size(FAR)
    share = rows // groups
    first = quarter_of(order) * rows
    holder = lax.axis_index(LIGHT)
    if order < 2:
        holder = partner(holder, 1)
    if order % 2 == 0:
        holder = partner(holder, 2)
    holder = holder // (lax.axis_size(LIGHT) // groups)
    onward = 1 - 2 * lax.axis_index("core")
    for at in range(0, rows, step):
        tex = tex_ref[pl.ds(pl.multiple_of(first + at, step), step), :]
        tile = sine(dot(tex, light_ref[...], (1, 1))).astype(BF16)
        tile_ref[order * rows + at : order * rows + at + step, :] = tile
        part = dot(tile, sketch_ref[...], (1, 0))
        for i in range(step // share):
            turn = (onward * (at // share + i - holder) + groups) % groups
            part_ref[pl.ds(pl.multiple_of(turn * share, share), share), :] = part[i * share : (i + 1) * share, :]


def tile_call(order, tex, light, sketch, *tiles):
    rows, lights, width = tex.shape[0] // 4, light.shape[0], sketch.shape[1]
    return on_core(
        functools.partial(tile_kernel, order=order),
        (jax.ShapeDtypeStruct((tex.shape[0], lights), BF16), jax.ShapeDtypeStruct((rows, width), F32)),
        "tile_quarter",
        flops=2 * rows * lights * (tex.shape[1] + width),
        aliases={3: 0} if tiles else None,
    )(tex, light, sketch, *tiles)


def mask_kernel(counts_ref, quarter_ref, rows_ref):
    rows = quarter_ref.shape[0]
    texel = lax.broadcasted_iota(jnp.int32, counts_ref.shape, 1)
    count = jnp.sum(jnp.where(texel == lax.axis_index(TEXEL), counts_ref[...], 0), axis=1, keepdims=True)
    row = lax.broadcasted_iota(jnp.int32, quarter_ref.shape, 0)
    rows_ref[...] = jnp.where(row + quarter_of(3) * rows < count, quarter_ref[...], 0.0)


def gram_kernel(rows_ref, gram_ref):
    parts = split(rows_ref[...])
    gram_ref[...] = dot_split(parts, parts, (0, 0))


def invert_factor(gram, y_ref, a_ref, w_ref):
    size = gram.shape[0]
    row = lax.broadcasted_iota(jnp.int32, (size, size), 0)
    col = lax.broadcasted_iota(jnp.int32, (size, size), 1)

    def lower_half(rest):
        return jnp.where(row > col, rest, jnp.where(row == col, 0.5 * rest, 0.0))

    diagonal = jnp.where(row == col, gram, 0.0)
    across_columns = lax.rsqrt(jnp.sum(diagonal, axis=0, keepdims=True))
    down_rows = lax.rsqrt(jnp.sum(diagonal, axis=1, keepdims=True))
    unit = jnp.where(row == col, F32(1), F32(0))
    a_ref[...] = gram
    y_ref[...] = (unit - lower_half(gram * down_rows * across_columns - unit)) * across_columns

    def refine(exact):
        y = y_ref[...]
        if exact:
            parts = split(y)
            rest = dot_split(split(dot_split(parts, split(a_ref[...]), (1, 0))), parts, (1, 1)) - unit
            y_ref[...] = y - dot_split(split(lower_half(rest)), parts, (1, 0))
        else:
            rough = y.astype(BF16)
            rest = dot(dot(rough, a_ref[...].astype(BF16), (1, 0)).astype(BF16), rough, (1, 1)) - unit
            y_ref[...] = y - dot(lower_half(rest).astype(BF16), rough, (1, 0))
        return jnp.sum(rest * rest)

    def steps(exact, enough):
        return lax.while_loop(
            lambda state: (state[0] < 8) & (state[1] > enough),
            lambda state: (state[0] + 1, refine(exact)),
            (jnp.int32(0), F32(1)),
        )[1]

    steps(False, 1e-1)
    rest = steps(True, 4e-6)

    @pl.when(jnp.logical_not(rest <= 4e-6))
    def _():
        y_ref[...] = unit
        line = lax.broadcasted_iota(jnp.int32, (size, 1), 0)
        w_ref[...] = gram

        def eliminate(j, carry):
            work = w_ref[...]
            column = jnp.sum(jnp.where(col == j, work, 0.0), axis=1, keepdims=True)
            pivot = lax.rsqrt(jnp.sum(jnp.where(line == j, column, 0.0), axis=0, keepdims=True))
            top = w_ref[pl.ds(j, 1), :] * pivot
            top_y = y_ref[pl.ds(j, 1), :] * pivot
            factor = jnp.where(line > j, column * pivot, 0.0)
            w_ref[...] = work - factor * top
            y_ref[...] = jnp.where(line == j, top_y, y_ref[...] - factor * top_y)
            return carry

        lax.fori_loop(0, size, eliminate, 0)


def basis_kernel(total_ref, gram_ref, *refs):
    quarter_refs, tile_ref = refs[:4], refs[4]
    basis_ref, keep_ref, send_ref, inverse_ref, a_ref, w_ref, half_ref, coeff_ref = refs[5:]
    total = total_ref[...]
    invert_factor(gram_ref[...] / total, inverse_ref, a_ref, w_ref)
    rows = basis_ref.shape[0] // 4
    inverse = split(inverse_ref[...])
    for order, ref in enumerate(quarter_refs):
        basis = dot_split(split(ref[...]), inverse, (1, 1))
        basis_ref[pl.ds(pl.multiple_of(quarter_of(order) * rows, rows), rows), :] = basis
        half_ref[order * rows : (order + 1) * rows, :] = basis.astype(BF16)
    coeffs = dot(half_ref[...], tile_ref[...], (0, 0))
    coeff_ref[...] = (coeffs * (1.0 / jnp.sqrt(total))).reshape(coeff_ref.shape)
    core = lax.axis_index("core")
    for i in range(keep_ref.shape[0]):
        keep_ref[i] = coeff_ref[2 * i + core]
        send_ref[i] = coeff_ref[2 * i + 1 - core]


def light_pairs(count, reach):
    pairs = []
    for core in range(2):
        shift = core * reach
        for z in range(count):
            pairs.append((core * count + z, core * count + ((((z - shift) % count) ^ reach) + shift) % count))
    return pairs


def across(value, reach):
    return lax.ppermute(value, ("core", *LIGHT), light_pairs(lax.axis_size(LIGHT), reach))


def onward(value, turn):
    count = lax.axis_size(LIGHT)
    pairs = [(c * count + z, c * count + (z + 4 * turn * (1 - 2 * c)) % count) for c in range(2) for z in range(count)]
    return lax.ppermute(value, ("core", *LIGHT), pairs)


def across_cores(value):
    return lax.ppermute(value, "core", [(0, 1), (1, 0)])


def each_to_each(parts, axes):
    return lax.all_to_all(parts, axes, 0, 0, tiled=True)


def to_each(value, axes):
    return each_to_each(jnp.broadcast_to(value, (lax.axis_size(axes), *value.shape)), axes)


def on_device(tex_feat, light_feat, sketch, row_counts):
    capacity, width = tex_feat.shape[0], sketch.shape[1]
    lights = light_feat.shape[0]
    texels, places = lax.axis_size(TEXEL), lax.axis_size(LIGHT)
    share_rows = capacity // places
    total = jnp.sum(row_counts).astype(F32).reshape(1, 1)

    inputs = (tex_feat, light_feat, sketch)
    tiles, part = tile_call(0, *inputs)
    passing = across(part, 1)
    tiles, turned = tile_call(2, *inputs, tiles)
    tiles, part = tile_call(1, *inputs, tiles)
    staying = across(part, 1)
    passed = across(turned + passing, 2)
    tiles, part = tile_call(3, *inputs, tiles)
    quarter = part + staying + passed
    own, following, opposite, previous = quarter.reshape(4, share_rows, width)
    arrived, third = onward(opposite, 1), onward(previous, -1)
    share = own + third + onward(following + arrived, 1)

    square = (width, width)
    quarter = lax.all_gather(share, FAR, axis=0, tiled=True)
    quarter = on_core(mask_kernel, jax.ShapeDtypeStruct(quarter.shape, F32), "used_rows")(
        row_counts.reshape(1, texels), quarter
    )
    near, beside = across(quarter, 2), across(quarter, 1)
    gram = on_core(gram_kernel, jax.ShapeDtypeStruct(square, F32), "gram_part")(quarter)
    gram_rows = jnp.sum(each_to_each(gram.reshape(texels, width // texels, width), TEXEL), axis=0)
    gram_rows, near, beside = lax.optimization_barrier((gram_rows, near, beside))
    beyond = across(near, 1)
    gram_rows = jnp.sum(to_each(gram_rows, ("z1", "z0")), axis=0)
    gram = to_each(gram_rows, TEXEL).reshape(square)

    lines, chips = width // texels, lax.axis_size(CHIP)
    basis, keep, send = on_core(
        basis_kernel,
        (
            jax.ShapeDtypeStruct((capacity, width), F32),
            jax.ShapeDtypeStruct((chips, lines, lights), F32),
            jax.ShapeDtypeStruct((chips, lines, lights), F32),
        ),
        "basis_and_coeffs",
        [pltpu.VMEM(square, F32)] * 3
        + [pltpu.VMEM((capacity, width), BF16), pltpu.VMEM((texels, lines, lights), F32)],
    )(total, gram, beyond, beside, near, quarter, tiles)
    mine = keep + across_cores(send)
    coeffs = jnp.sum(each_to_each(mine, CHIP), axis=0)
    return basis, coeffs


def solution(mesh):
    fine = Mesh(np.asarray(mesh.devices).reshape(4, 4, 2, 2, 2, 2, 2), (*TEXEL, *LIGHT))
    placed = (P(TEXEL, None), P(LIGHT, None), P(LIGHT, None), P())
    return jax.shard_map(
        on_device, mesh=fine, in_specs=placed, out_specs=(P(TEXEL, None), P(TEXEL, LIGHT)), check_vma=False
    )
```

```python
import functools
import math

import jax
import jax.numpy as jnp
import numpy as np
from jax import lax
from jax.experimental import pallas as pl
from jax.experimental.pallas import tpu as pltpu
from jax.sharding import Mesh, PartitionSpec as P

F32 = jnp.float32
BF16 = jnp.bfloat16
CHIP = ("x", "y")
TEXEL = CHIP + ("core",)
FAR = ("z3", "z2")
LIGHT = FAR + ("z1", "z0")
HIGHEST = lax.Precision.HIGHEST
VMEM_LIMIT = 24 * 2**20


def sine_coefficients():
    angle = (np.arange(4000) + 0.5) * math.pi / 4000
    u = 0.125 * (1 + np.cos(angle)) + 1e-9
    w = 1.0
    basis = np.stack([u ** (2 * i + 1) for i in range(5)], axis=1)
    fit, *_ = np.linalg.lstsq(basis / w, np.sin(2 * math.pi * u) / w, rcond=None)
    return [float(c) for c in fit]


SINE = sine_coefficients()
ROUNDER = float(1.5 * 2**23)


def sine(x):
    turns = x * F32(1 / (2 * math.pi))
    part = turns - ((turns + F32(ROUNDER)) - F32(ROUNDER))
    part = jnp.maximum(jnp.minimum(part, F32(0.5) - part), F32(-0.5) - part)
    sq = part * part
    value = F32(SINE[4])
    for c in SINE[3::-1]:
        value = value * sq + F32(c)
    return value * part


def dot(a, b, contract, precision=None):
    return lax.dot_general(
        a, b, ((contract[0:1], contract[1:2]), ((), ())), precision=precision, preferred_element_type=F32
    )


VMEM = pl.BlockSpec(memory_space=pltpu.VMEM)


def on_core(kernel, out_shape, name, scratch=(), flops=10**9, aliases=None):
    call = lambda *operands: pl.pallas_call(
        kernel,
        out_shape=out_shape,
        in_specs=[VMEM] * len(operands),
        out_specs=jax.tree.map(lambda _: VMEM, out_shape),
        scratch_shapes=scratch,
        input_output_aliases=aliases or {},
        compiler_params=pltpu.CompilerParams(vmem_limit_bytes=VMEM_LIMIT),
        cost_estimate=pl.CostEstimate(flops=flops, bytes_accessed=2**20, transcendentals=0),
        name=name,
    )(*operands)
    return call


def quarter_of(order):
    low, second, core = (lax.axis_index(axis) for axis in ("z0", "z1", "core"))
    if order < 2:
        return 2 * (1 - low) + (second + core + 1 - order) % 2
    return 2 * low + (second + 1 - (order - 2)) % 2


def partner(place, reach):
    places, shift = lax.axis_size(LIGHT), lax.axis_index("core") * reach
    return (((place - shift + places) % places ^ reach) + shift) % places


def split(value):
    high = value.astype(BF16)
    return high, (value - high.astype(F32)).astype(BF16)


def dot_split(a, b, contract):
    (a_high, a_low), (b_high, b_low) = a, b
    return dot(a_high, b_high, contract) + (dot(a_high, b_low, contract) + dot(a_low, b_high, contract))


def tile_kernel(tex_ref, light_ref, sketch_ref, *refs, order, step=128):
    tile_ref, part_ref = refs[-2:]
    rows, groups = part_ref.shape[0], lax.axis_size(FAR)
    share = rows // groups
    first = quarter_of(order) * rows
    holder = lax.axis_index(LIGHT)
    if order < 2:
        holder = partner(holder, 1)
    if order % 2 == 0:
        holder = partner(holder, 2)
    holder = holder // (lax.axis_size(LIGHT) // groups)
    onward = 1 - 2 * lax.axis_index("core")
    for at in range(0, rows, step):
        tex = tex_ref[pl.ds(pl.multiple_of(first + at, step), step), :]
        tile = sine(dot(tex, light_ref[...], (1, 1))).astype(BF16)
        tile_ref[order * rows + at : order * rows + at + step, :] = tile
        part = dot(tile, sketch_ref[...], (1, 0))
        for i in range(step // share):
            turn = (onward * (at // share + i - holder) + groups) % groups
            part_ref[pl.ds(pl.multiple_of(turn * share, share), share), :] = part[i * share : (i + 1) * share, :]


def tile_call(order, tex, light, sketch, *tiles):
    rows, lights, width = tex.shape[0] // 4, light.shape[0], sketch.shape[1]
    return on_core(
        functools.partial(tile_kernel, order=order),
        (jax.ShapeDtypeStruct((tex.shape[0], lights), BF16), jax.ShapeDtypeStruct((rows, width), F32)),
        "tile_quarter",
        flops=2 * rows * lights * (tex.shape[1] + width),
        aliases={3: 0} if tiles else None,
    )(tex, light, sketch, *tiles)


def mask_kernel(counts_ref, quarter_ref, rows_ref):
    rows = quarter_ref.shape[0]
    texel = lax.broadcasted_iota(jnp.int32, counts_ref.shape, 1)
    count = jnp.sum(jnp.where(texel == lax.axis_index(TEXEL), counts_ref[...], 0), axis=1, keepdims=True)
    row = lax.broadcasted_iota(jnp.int32, quarter_ref.shape, 0)
    rows_ref[...] = jnp.where(row + quarter_of(3) * rows < count, quarter_ref[...], 0.0)


def gram_kernel(rows_ref, gram_ref):
    parts = split(rows_ref[...])
    gram_ref[...] = dot_split(parts, parts, (0, 0))


def invert_factor(gram, y_ref, a_ref, w_ref):
    size = gram.shape[0]
    row = lax.broadcasted_iota(jnp.int32, (size, size), 0)
    col = lax.broadcasted_iota(jnp.int32, (size, size), 1)

    def lower_half(rest):
        return jnp.where(row > col, rest, jnp.where(row == col, 0.5 * rest, 0.0))

    diagonal = jnp.where(row == col, gram, 0.0)
    across_columns = lax.rsqrt(jnp.sum(diagonal, axis=0, keepdims=True))
    down_rows = lax.rsqrt(jnp.sum(diagonal, axis=1, keepdims=True))
    unit = jnp.where(row == col, F32(1), F32(0))
    a_ref[...] = gram
    y_ref[...] = (unit - lower_half(gram * down_rows * across_columns - unit)) * across_columns

    def refine(exact):
        y = y_ref[...]
        if exact:
            parts = split(y)
            rest = dot_split(split(dot_split(parts, split(a_ref[...]), (1, 0))), parts, (1, 1)) - unit
            y_ref[...] = y - dot_split(split(lower_half(rest)), parts, (1, 0))
        else:
            rough = y.astype(BF16)
            rest = dot(dot(rough, a_ref[...].astype(BF16), (1, 0)).astype(BF16), rough, (1, 1)) - unit
            y_ref[...] = y - dot(lower_half(rest).astype(BF16), rough, (1, 0))
        return jnp.sum(rest * rest)

    def steps(exact, enough):
        return lax.while_loop(
            lambda state: (state[0] < 8) & (state[1] > enough),
            lambda state: (state[0] + 1, refine(exact)),
            (jnp.int32(0), F32(1)),
        )[1]

    steps(False, 1e-1)
    rest = steps(True, 4e-6)

    @pl.when(jnp.logical_not(rest <= 4e-6))
    def _():
        y_ref[...] = unit
        line = lax.broadcasted_iota(jnp.int32, (size, 1), 0)
        w_ref[...] = gram

        def eliminate(j, carry):
            work = w_ref[...]
            column = jnp.sum(jnp.where(col == j, work, 0.0), axis=1, keepdims=True)
            pivot = lax.rsqrt(jnp.sum(jnp.where(line == j, column, 0.0), axis=0, keepdims=True))
            top = w_ref[pl.ds(j, 1), :] * pivot
            top_y = y_ref[pl.ds(j, 1), :] * pivot
            factor = jnp.where(line > j, column * pivot, 0.0)
            w_ref[...] = work - factor * top
            y_ref[...] = jnp.where(line == j, top_y, y_ref[...] - factor * top_y)
            return carry

        lax.fori_loop(0, size, eliminate, 0)


def basis_kernel(total_ref, gram_ref, *refs):
    quarter_refs, tile_ref = refs[:4], refs[4]
    basis_ref, keep_ref, send_ref, inverse_ref, a_ref, w_ref, half_ref, coeff_ref = refs[5:]
    total = total_ref[...]
    invert_factor(gram_ref[...] / total, inverse_ref, a_ref, w_ref)
    rows = basis_ref.shape[0] // 4
    inverse = split(inverse_ref[...])
    for order, ref in enumerate(quarter_refs):
        basis = dot_split(split(ref[...]), inverse, (1, 1))
        basis_ref[pl.ds(pl.multiple_of(quarter_of(order) * rows, rows), rows), :] = basis
        half_ref[order * rows : (order + 1) * rows, :] = basis.astype(BF16)
    coeffs = dot(half_ref[...], tile_ref[...], (0, 0))
    coeff_ref[...] = (coeffs * (1.0 / jnp.sqrt(total))).reshape(coeff_ref.shape)
    core = lax.axis_index("core")
    for i in range(keep_ref.shape[0]):
        keep_ref[i] = coeff_ref[2 * i + core]
        send_ref[i] = coeff_ref[2 * i + 1 - core]


def light_pairs(count, reach):
    pairs = []
    for core in range(2):
        shift = core * reach
        for z in range(count):
            pairs.append((core * count + z, core * count + ((((z - shift) % count) ^ reach) + shift) % count))
    return pairs


def across(value, reach):
    return lax.ppermute(value, ("core", *LIGHT), light_pairs(lax.axis_size(LIGHT), reach))


def onward(value, turn):
    count = lax.axis_size(LIGHT)
    pairs = [(c * count + z, c * count + (z + 4 * turn * (1 - 2 * c)) % count) for c in range(2) for z in range(count)]
    return lax.ppermute(value, ("core", *LIGHT), pairs)


def across_cores(value):
    return lax.ppermute(value, "core", [(0, 1), (1, 0)])


def each_to_each(parts, axes):
    return lax.all_to_all(parts, axes, 0, 0, tiled=True)


def to_each(value, axes):
    return each_to_each(jnp.broadcast_to(value, (lax.axis_size(axes), *value.shape)), axes)


def on_device(tex_feat, light_feat, sketch, row_counts):
    capacity, width = tex_feat.shape[0], sketch.shape[1]
    lights = light_feat.shape[0]
    texels, places = lax.axis_size(TEXEL), lax.axis_size(LIGHT)
    share_rows = capacity // places
    total = jnp.sum(row_counts).astype(F32).reshape(1, 1)

    inputs = (tex_feat, light_feat, sketch)
    tiles, part = tile_call(0, *inputs)
    passing = across(part, 1)
    tiles, turned = tile_call(2, *inputs, tiles)
    tiles, part = tile_call(1, *inputs, tiles)
    staying = across(part, 1)
    passed = across(turned + passing, 2)
    tiles, part = tile_call(3, *inputs, tiles)
    quarter = part + staying + passed
    own, following, opposite, previous = quarter.reshape(4, share_rows, width)
    arrived, third = onward(opposite, 1), onward(previous, -1)
    share = own + third + onward(following + arrived, 1)

    square = (width, width)
    quarter = lax.all_gather(share, FAR, axis=0, tiled=True)
    quarter = on_core(mask_kernel, jax.ShapeDtypeStruct(quarter.shape, F32), "used_rows")(
        row_counts.reshape(1, texels), quarter
    )
    near = across(quarter, 2)
    gram = on_core(gram_kernel, jax.ShapeDtypeStruct(square, F32), "gram_part")(quarter)
    gram_rows = jnp.sum(each_to_each(gram.reshape(texels, width // texels, width), TEXEL), axis=0)
    gram_rows, near, quarter = lax.optimization_barrier((gram_rows, near, quarter))
    beyond, beside = across(near, 1), across(quarter, 1)
    gram_rows = jnp.sum(to_each(gram_rows, ("z1", "z0")), axis=0)
    gram = to_each(gram_rows, TEXEL).reshape(square)

    lines, chips = width // texels, lax.axis_size(CHIP)
    basis, keep, send = on_core(
        basis_kernel,
        (
            jax.ShapeDtypeStruct((capacity, width), F32),
            jax.ShapeDtypeStruct((chips, lines, lights), F32),
            jax.ShapeDtypeStruct((chips, lines, lights), F32),
        ),
        "basis_and_coeffs",
        [pltpu.VMEM(square, F32)] * 3
        + [pltpu.VMEM((capacity, width), BF16), pltpu.VMEM((texels, lines, lights), F32)],
    )(total, gram, beyond, beside, near, quarter, tiles)
    mine = keep + across_cores(send)
    coeffs = jnp.sum(each_to_each(mine, CHIP), axis=0)
    return basis, coeffs


def solution(mesh):
    fine = Mesh(np.asarray(mesh.devices).reshape(4, 4, 2, 2, 2, 2, 2), (*TEXEL, *LIGHT))
    placed = (P(TEXEL, None), P(LIGHT, None), P(LIGHT, None), P())
    return jax.shard_map(
        on_device, mesh=fine, in_specs=placed, out_specs=(P(TEXEL, None), P(TEXEL, LIGHT)), check_vma=False
    )
```

```python
import functools
import math

import jax
import jax.numpy as jnp
import numpy as np
from jax import lax
from jax.experimental import pallas as pl
from jax.experimental.pallas import tpu as pltpu
from jax.sharding import Mesh, PartitionSpec as P

F32 = jnp.float32
BF16 = jnp.bfloat16
CHIP = ("x", "y")
TEXEL = CHIP + ("core",)
FAR = ("z3", "z2")
LIGHT = FAR + ("z1", "z0")
HIGHEST = lax.Precision.HIGHEST
VMEM_LIMIT = 24 * 2**20


def sine_coefficients():
    angle = (np.arange(4000) + 0.5) * math.pi / 4000
    u = 0.125 * (1 + np.cos(angle)) + 1e-9
    w = 1.0
    basis = np.stack([u ** (2 * i + 1) for i in range(5)], axis=1)
    fit, *_ = np.linalg.lstsq(basis / w, np.sin(2 * math.pi * u) / w, rcond=None)
    return [float(c) for c in fit]


SINE = sine_coefficients()
ROUNDER = float(1.5 * 2**23)


def sine(x):
    turns = x * F32(1 / (2 * math.pi))
    part = turns - ((turns + F32(ROUNDER)) - F32(ROUNDER))
    part = jnp.maximum(jnp.minimum(part, F32(0.5) - part), F32(-0.5) - part)
    sq = part * part
    value = F32(SINE[4])
    for c in SINE[3::-1]:
        value = value * sq + F32(c)
    return value * part


def dot(a, b, contract, precision=None):
    return lax.dot_general(
        a, b, ((contract[0:1], contract[1:2]), ((), ())), precision=precision, preferred_element_type=F32
    )


VMEM = pl.BlockSpec(memory_space=pltpu.VMEM)


def on_core(kernel, out_shape, name, scratch=(), flops=10**9, aliases=None):
    call = lambda *operands: pl.pallas_call(
        kernel,
        out_shape=out_shape,
        in_specs=[VMEM] * len(operands),
        out_specs=jax.tree.map(lambda _: VMEM, out_shape),
        scratch_shapes=scratch,
        input_output_aliases=aliases or {},
        compiler_params=pltpu.CompilerParams(vmem_limit_bytes=VMEM_LIMIT),
        cost_estimate=pl.CostEstimate(flops=flops, bytes_accessed=2**20, transcendentals=0),
        name=name,
    )(*operands)
    return call


def quarter_of(order):
    low, second, core = (lax.axis_index(axis) for axis in ("z0", "z1", "core"))
    if order < 2:
        return 2 * (1 - low) + (second + core + 1 - order) % 2
    return 2 * low + (second + 1 - (order - 2)) % 2


def partner(place, reach):
    places, shift = lax.axis_size(LIGHT), lax.axis_index("core") * reach
    return (((place - shift + places) % places ^ reach) + shift) % places


def split(value):
    high = value.astype(BF16)
    return high, (value - high.astype(F32)).astype(BF16)


def dot_split(a, b, contract):
    (a_high, a_low), (b_high, b_low) = a, b
    return dot(a_high, b_high, contract) + (dot(a_high, b_low, contract) + dot(a_low, b_high, contract))


def tile_kernel(tex_ref, light_ref, sketch_ref, *refs, order, step=128):
    tile_ref, part_ref = refs[-2:]
    rows, groups = part_ref.shape[0], lax.axis_size(FAR)
    share = rows // groups
    first = quarter_of(order) * rows
    holder = lax.axis_index(LIGHT)
    if order < 2:
        holder = partner(holder, 1)
    if order % 2 == 0:
        holder = partner(holder, 2)
    holder = holder // (lax.axis_size(LIGHT) // groups)
    onward = 1 - 2 * lax.axis_index("core")
    for at in range(0, rows, step):
        tex = tex_ref[pl.ds(pl.multiple_of(first + at, step), step), :]
        tile = sine(dot(tex, light_ref[...], (1, 1))).astype(BF16)
        tile_ref[order * rows + at : order * rows + at + step, :] = tile
        part = dot(tile, sketch_ref[...], (1, 0))
        for i in range(step // share):
            turn = (onward * (at // share + i - holder) + groups) % groups
            part_ref[pl.ds(pl.multiple_of(turn * share, share), share), :] = part[i * share : (i + 1) * share, :]


def tile_call(order, tex, light, sketch, *tiles):
    rows, lights, width = tex.shape[0] // 4, light.shape[0], sketch.shape[1]
    return on_core(
        functools.partial(tile_kernel, order=order),
        (jax.ShapeDtypeStruct((tex.shape[0], lights), BF16), jax.ShapeDtypeStruct((rows, width), F32)),
        "tile_quarter",
        flops=2 * rows * lights * (tex.shape[1] + width),
        aliases={3: 0} if tiles else None,
    )(tex, light, sketch, *tiles)


def used(counts_ref, order, shape):
    texel = lax.broadcasted_iota(jnp.int32, counts_ref.shape, 1)
    count = jnp.sum(jnp.where(texel == lax.axis_index(TEXEL), counts_ref[...], 0), axis=1, keepdims=True)
    return lax.broadcasted_iota(jnp.int32, shape, 0) + quarter_of(order) * shape[0] < count


def gram_kernel(counts_ref, quarter_ref, gram_ref):
    parts = split(jnp.where(used(counts_ref, 3, quarter_ref.shape), quarter_ref[...], 0.0))
    gram_ref[...] = dot_split(parts, parts, (0, 0))


def invert_factor(gram, y_ref, a_ref, w_ref):
    size = gram.shape[0]
    row = lax.broadcasted_iota(jnp.int32, (size, size), 0)
    col = lax.broadcasted_iota(jnp.int32, (size, size), 1)

    def lower_half(rest):
        return jnp.where(row > col, rest, jnp.where(row == col, 0.5 * rest, 0.0))

    diagonal = jnp.where(row == col, gram, 0.0)
    across_columns = lax.rsqrt(jnp.sum(diagonal, axis=0, keepdims=True))
    down_rows = lax.rsqrt(jnp.sum(diagonal, axis=1, keepdims=True))
    unit = jnp.where(row == col, F32(1), F32(0))
    a_ref[...] = gram
    y_ref[...] = (unit - lower_half(gram * down_rows * across_columns - unit)) * across_columns

    def refine(exact):
        y = y_ref[...]
        if exact:
            parts = split(y)
            rest = dot_split(split(dot_split(parts, split(a_ref[...]), (1, 0))), parts, (1, 1)) - unit
            y_ref[...] = y - dot_split(split(lower_half(rest)), parts, (1, 0))
        else:
            rough = y.astype(BF16)
            rest = dot(dot(rough, a_ref[...].astype(BF16), (1, 0)).astype(BF16), rough, (1, 1)) - unit
            y_ref[...] = y - dot(lower_half(rest).astype(BF16), rough, (1, 0))
        return jnp.sum(rest * rest)

    def steps(exact, enough):
        return lax.while_loop(
            lambda state: (state[0] < 8) & (state[1] > enough),
            lambda state: (state[0] + 1, refine(exact)),
            (jnp.int32(0), F32(1)),
        )[1]

    steps(False, 1e-1)
    rest = steps(True, 4e-6)

    @pl.when(jnp.logical_not(rest <= 4e-6))
    def _():
        y_ref[...] = unit
        line = lax.broadcasted_iota(jnp.int32, (size, 1), 0)
        w_ref[...] = gram

        def eliminate(j, carry):
            work = w_ref[...]
            column = jnp.sum(jnp.where(col == j, work, 0.0), axis=1, keepdims=True)
            pivot = lax.rsqrt(jnp.sum(jnp.where(line == j, column, 0.0), axis=0, keepdims=True))
            top = w_ref[pl.ds(j, 1), :] * pivot
            top_y = y_ref[pl.ds(j, 1), :] * pivot
            factor = jnp.where(line > j, column * pivot, 0.0)
            w_ref[...] = work - factor * top
            y_ref[...] = jnp.where(line == j, top_y, y_ref[...] - factor * top_y)
            return carry

        lax.fori_loop(0, size, eliminate, 0)


def basis_kernel(counts_ref, gram_ref, *refs):
    quarter_refs, tile_ref = refs[:4], refs[4]
    basis_ref, keep_ref, send_ref, inverse_ref, a_ref, w_ref, half_ref, coeff_ref = refs[5:]
    total = jnp.sum(counts_ref[...].astype(F32), axis=1, keepdims=True)
    invert_factor(gram_ref[...] / total, inverse_ref, a_ref, w_ref)
    rows = basis_ref.shape[0] // 4
    inverse = split(inverse_ref[...])
    for order, ref in enumerate(quarter_refs):
        basis = jnp.where(used(counts_ref, order, ref.shape), dot_split(split(ref[...]), inverse, (1, 1)), 0.0)
        basis_ref[pl.ds(pl.multiple_of(quarter_of(order) * rows, rows), rows), :] = basis
        half_ref[order * rows : (order + 1) * rows, :] = basis.astype(BF16)
    coeffs = dot(half_ref[...], tile_ref[...], (0, 0))
    coeff_ref[...] = (coeffs * (1.0 / jnp.sqrt(total))).reshape(coeff_ref.shape)
    core = lax.axis_index("core")
    for i in range(keep_ref.shape[0]):
        keep_ref[i] = coeff_ref[2 * i + core]
        send_ref[i] = coeff_ref[2 * i + 1 - core]


def light_pairs(count, reach):
    pairs = []
    for core in range(2):
        shift = core * reach
        for z in range(count):
            pairs.append((core * count + z, core * count + ((((z - shift) % count) ^ reach) + shift) % count))
    return pairs


def across(value, reach):
    return lax.ppermute(value, ("core", *LIGHT), light_pairs(lax.axis_size(LIGHT), reach))


def onward(value, turn):
    count = lax.axis_size(LIGHT)
    pairs = [(c * count + z, c * count + (z + 4 * turn * (1 - 2 * c)) % count) for c in range(2) for z in range(count)]
    return lax.ppermute(value, ("core", *LIGHT), pairs)


def across_cores(value):
    return lax.ppermute(value, "core", [(0, 1), (1, 0)])


def each_to_each(parts, axes):
    return lax.all_to_all(parts, axes, 0, 0, tiled=True)


def to_each(value, axes):
    return each_to_each(jnp.broadcast_to(value, (lax.axis_size(axes), *value.shape)), axes)


def on_device(tex_feat, light_feat, sketch, row_counts):
    capacity, width = tex_feat.shape[0], sketch.shape[1]
    lights = light_feat.shape[0]
    texels, places = lax.axis_size(TEXEL), lax.axis_size(LIGHT)
    share_rows = capacity // places
    counts = row_counts.reshape(1, texels)

    inputs = (tex_feat, light_feat, sketch)
    tiles, part = tile_call(0, *inputs)
    passing = across(part, 1)
    tiles, turned = tile_call(2, *inputs, tiles)
    tiles, part = tile_call(1, *inputs, tiles)
    staying = across(part, 1)
    passed = across(turned + passing, 2)
    tiles, part = tile_call(3, *inputs, tiles)
    quarter = part + staying + passed
    own, following, opposite, previous = quarter.reshape(4, share_rows, width)
    arrived, third = onward(opposite, 1), onward(previous, -1)
    share = own + third + onward(following + arrived, 1)

    square = (width, width)
    quarter = lax.all_gather(share, FAR, axis=0, tiled=True)
    near = across(quarter, 2)
    gram = on_core(gram_kernel, jax.ShapeDtypeStruct(square, F32), "gram_part")(counts, quarter)
    gram_rows = jnp.sum(each_to_each(gram.reshape(texels, width // texels, width), TEXEL), axis=0)
    gram_rows, near, quarter = lax.optimization_barrier((gram_rows, near, quarter))
    beyond, beside = across(near, 1), across(quarter, 1)
    gram_rows = jnp.sum(to_each(gram_rows, ("z1", "z0")), axis=0)
    gram = to_each(gram_rows, TEXEL).reshape(square)

    lines, chips = width // texels, lax.axis_size(CHIP)
    basis, keep, send = on_core(
        basis_kernel,
        (
            jax.ShapeDtypeStruct((capacity, width), F32),
            jax.ShapeDtypeStruct((chips, lines, lights), F32),
            jax.ShapeDtypeStruct((chips, lines, lights), F32),
        ),
        "basis_and_coeffs",
        [pltpu.VMEM(square, F32)] * 3
        + [pltpu.VMEM((capacity, width), BF16), pltpu.VMEM((texels, lines, lights), F32)],
    )(counts, gram, beyond, beside, near, quarter, tiles)
    mine = keep + across_cores(send)
    coeffs = jnp.sum(each_to_each(mine, CHIP), axis=0)
    return basis, coeffs


def solution(mesh):
    fine = Mesh(np.asarray(mesh.devices).reshape(4, 4, 2, 2, 2, 2, 2), (*TEXEL, *LIGHT))
    placed = (P(TEXEL, None), P(LIGHT, None), P(LIGHT, None), P())
    return jax.shard_map(
        on_device, mesh=fine, in_specs=placed, out_specs=(P(TEXEL, None), P(TEXEL, LIGHT)), check_vma=False
    )
```

```python
import functools
import math

import jax
import jax.numpy as jnp
import numpy as np
from jax import lax
from jax.experimental import pallas as pl
from jax.experimental.pallas import tpu as pltpu
from jax.sharding import Mesh, PartitionSpec as P

F32 = jnp.float32
BF16 = jnp.bfloat16
CHIP = ("x", "y")
TEXEL = CHIP + ("core",)
FAR = ("z3", "z2")
LIGHT = FAR + ("z1", "z0")
HIGHEST = lax.Precision.HIGHEST
VMEM_LIMIT = 24 * 2**20


def sine_coefficients():
    angle = (np.arange(4000) + 0.5) * math.pi / 4000
    u = 0.125 * (1 + np.cos(angle)) + 1e-9
    w = 1.0
    basis = np.stack([u ** (2 * i + 1) for i in range(5)], axis=1)
    fit, *_ = np.linalg.lstsq(basis / w, np.sin(2 * math.pi * u) / w, rcond=None)
    return [float(c) for c in fit]


SINE = sine_coefficients()
ROUNDER = float(1.5 * 2**23)


def sine(x):
    turns = x * F32(1 / (2 * math.pi))
    part = turns - ((turns + F32(ROUNDER)) - F32(ROUNDER))
    part = jnp.maximum(jnp.minimum(part, F32(0.5) - part), F32(-0.5) - part)
    sq = part * part
    value = F32(SINE[4])
    for c in SINE[3::-1]:
        value = value * sq + F32(c)
    return value * part


def dot(a, b, contract, precision=None):
    return lax.dot_general(
        a, b, ((contract[0:1], contract[1:2]), ((), ())), precision=precision, preferred_element_type=F32
    )


VMEM = pl.BlockSpec(memory_space=pltpu.VMEM)


def on_core(kernel, out_shape, name, scratch=(), flops=10**9, aliases=None):
    call = lambda *operands: pl.pallas_call(
        kernel,
        out_shape=out_shape,
        in_specs=[VMEM] * len(operands),
        out_specs=jax.tree.map(lambda _: VMEM, out_shape),
        scratch_shapes=scratch,
        input_output_aliases=aliases or {},
        compiler_params=pltpu.CompilerParams(vmem_limit_bytes=VMEM_LIMIT),
        cost_estimate=pl.CostEstimate(flops=flops, bytes_accessed=2**20, transcendentals=0),
        name=name,
    )(*operands)
    return call


def quarter_of(order):
    low, second, core = (lax.axis_index(axis) for axis in ("z0", "z1", "core"))
    if order < 2:
        return 2 * (1 - low) + (second + core + 1 - order) % 2
    return 2 * low + (second + 1 - (order - 2)) % 2


def partner(place, reach):
    places, shift = lax.axis_size(LIGHT), lax.axis_index("core") * reach
    return (((place - shift + places) % places ^ reach) + shift) % places


def split(value):
    high = value.astype(BF16)
    return high, (value - high.astype(F32)).astype(BF16)


def dot_split(a, b, contract):
    (a_high, a_low), (b_high, b_low) = a, b
    return dot(a_high, b_high, contract) + (dot(a_high, b_low, contract) + dot(a_low, b_high, contract))


def tile_kernel(tex_ref, light_ref, sketch_ref, *refs, order, step=128):
    tile_ref, part_ref = refs[-2:]
    rows, groups = part_ref.shape[0], lax.axis_size(FAR)
    share = rows // groups
    first = quarter_of(order) * rows
    holder = lax.axis_index(LIGHT)
    if order < 2:
        holder = partner(holder, 1)
    if order % 2 == 0:
        holder = partner(holder, 2)
    holder = holder // (lax.axis_size(LIGHT) // groups)
    onward = 1 - 2 * lax.axis_index("core")
    for at in range(0, rows, step):
        tex = tex_ref[pl.ds(pl.multiple_of(first + at, step), step), :]
        tile = sine(dot(tex, light_ref[...], (1, 1))).astype(BF16)
        tile_ref[order * rows + at : order * rows + at + step, :] = tile
        part = dot(tile, sketch_ref[...], (1, 0))
        for i in range(step // share):
            turn = (onward * (at // share + i - holder) + groups) % groups
            part_ref[pl.ds(pl.multiple_of(turn * share, share), share), :] = part[i * share : (i + 1) * share, :]


def tile_call(order, tex, light, sketch, *tiles):
    rows, lights, width = tex.shape[0] // 4, light.shape[0], sketch.shape[1]
    return on_core(
        functools.partial(tile_kernel, order=order),
        (jax.ShapeDtypeStruct((tex.shape[0], lights), BF16), jax.ShapeDtypeStruct((rows, width), F32)),
        "tile_quarter",
        flops=2 * rows * lights * (tex.shape[1] + width),
        aliases={3: 0} if tiles else None,
    )(tex, light, sketch, *tiles)


def used(counts_ref, order, shape):
    texel = lax.broadcasted_iota(jnp.int32, counts_ref.shape, 1)
    count = jnp.sum(jnp.where(texel == lax.axis_index(TEXEL), counts_ref[...], 0), axis=1, keepdims=True)
    return lax.broadcasted_iota(jnp.int32, shape, 0) + quarter_of(order) * shape[0] < count


def gram_kernel(counts_ref, quarter_ref, gram_ref):
    parts = split(jnp.where(used(counts_ref, 3, quarter_ref.shape), quarter_ref[...], 0.0))
    gram_ref[...] = dot_split(parts, parts, (0, 0))


def invert_factor(gram, y_ref, a_ref, w_ref):
    size = gram.shape[0]
    row = lax.broadcasted_iota(jnp.int32, (size, size), 0)
    col = lax.broadcasted_iota(jnp.int32, (size, size), 1)

    def lower_half(rest):
        return jnp.where(row > col, rest, jnp.where(row == col, 0.5 * rest, 0.0))

    diagonal = jnp.where(row == col, gram, 0.0)
    across_columns = lax.rsqrt(jnp.sum(diagonal, axis=0, keepdims=True))
    down_rows = lax.rsqrt(jnp.sum(diagonal, axis=1, keepdims=True))
    unit = jnp.where(row == col, F32(1), F32(0))
    a_ref[...] = gram
    y_ref[...] = (unit - lower_half(gram * down_rows * across_columns - unit)) * across_columns

    def refine(exact):
        y = y_ref[...]
        if exact:
            parts = split(y)
            rest = dot_split(split(dot_split(parts, split(a_ref[...]), (1, 0))), parts, (1, 1)) - unit
            y_ref[...] = y - dot_split(split(lower_half(rest)), parts, (1, 0))
        else:
            rough = y.astype(BF16)
            rest = dot(dot(rough, a_ref[...].astype(BF16), (1, 0)).astype(BF16), rough, (1, 1)) - unit
            y_ref[...] = y - dot(lower_half(rest).astype(BF16), rough, (1, 0))
        return jnp.sum(rest * rest)

    def steps(exact, enough):
        return lax.while_loop(
            lambda state: (state[0] < 8) & (state[1] > enough),
            lambda state: (state[0] + 1, refine(exact)),
            (jnp.int32(0), F32(1)),
        )[1]

    steps(False, 1e-1)
    rest = steps(True, 4e-6)

    @pl.when(jnp.logical_not(rest <= 4e-6))
    def _():
        y_ref[...] = unit
        line = lax.broadcasted_iota(jnp.int32, (size, 1), 0)
        w_ref[...] = gram

        def eliminate(j, carry):
            work = w_ref[...]
            column = jnp.sum(jnp.where(col == j, work, 0.0), axis=1, keepdims=True)
            pivot = lax.rsqrt(jnp.sum(jnp.where(line == j, column, 0.0), axis=0, keepdims=True))
            top = w_ref[pl.ds(j, 1), :] * pivot
            top_y = y_ref[pl.ds(j, 1), :] * pivot
            factor = jnp.where(line > j, column * pivot, 0.0)
            w_ref[...] = work - factor * top
            y_ref[...] = jnp.where(line == j, top_y, y_ref[...] - factor * top_y)
            return carry

        lax.fori_loop(0, size, eliminate, 0)


def basis_kernel(counts_ref, gram_ref, *refs):
    quarter_refs, tile_ref = refs[:4], refs[4]
    basis_ref, keep_ref, send_ref, inverse_ref, a_ref, w_ref, half_ref, coeff_ref = refs[5:]
    total = jnp.sum(counts_ref[...].astype(F32), axis=1, keepdims=True)
    invert_factor(gram_ref[...] / total, inverse_ref, a_ref, w_ref)
    rows = basis_ref.shape[0] // 4
    inverse = split(inverse_ref[...])
    for order, ref in enumerate(quarter_refs):
        basis = jnp.where(used(counts_ref, order, ref.shape), dot_split(split(ref[...]), inverse, (1, 1)), 0.0)
        basis_ref[pl.ds(pl.multiple_of(quarter_of(order) * rows, rows), rows), :] = basis
        half_ref[order * rows : (order + 1) * rows, :] = basis.astype(BF16)
    coeffs = dot(half_ref[...], tile_ref[...], (0, 0))
    coeff_ref[...] = (coeffs * (1.0 / jnp.sqrt(total))).reshape(coeff_ref.shape)
    core = lax.axis_index("core")
    for i in range(keep_ref.shape[0]):
        keep_ref[i] = coeff_ref[2 * i + core]
        send_ref[i] = coeff_ref[2 * i + 1 - core]


def light_pairs(count, reach):
    pairs = []
    for core in range(2):
        shift = core * reach
        for z in range(count):
            pairs.append((core * count + z, core * count + ((((z - shift) % count) ^ reach) + shift) % count))
    return pairs


def across(value, reach):
    return lax.ppermute(value, ("core", *LIGHT), light_pairs(lax.axis_size(LIGHT), reach))


def onward(value, turn):
    count = lax.axis_size(LIGHT)
    pairs = [(c * count + z, c * count + (z + 4 * turn * (1 - 2 * c)) % count) for c in range(2) for z in range(count)]
    return lax.ppermute(value, ("core", *LIGHT), pairs)


def across_cores(value):
    return lax.ppermute(value, "core", [(0, 1), (1, 0)])


def each_to_each(parts, axes):
    return lax.all_to_all(parts, axes, 0, 0, tiled=True)


def sum_kernel(parts_ref, copies_ref):
    copies_ref[...] = jnp.broadcast_to(jnp.sum(parts_ref[...], axis=0, keepdims=True), copies_ref.shape)


def sum_to_each(parts, axes):
    copies = jax.ShapeDtypeStruct((lax.axis_size(axes), *parts.shape[1:]), parts.dtype)
    return each_to_each(on_core(sum_kernel, copies, "sum_and_repeat")(parts), axes)


def on_device(tex_feat, light_feat, sketch, row_counts):
    capacity, width = tex_feat.shape[0], sketch.shape[1]
    lights = light_feat.shape[0]
    texels, places = lax.axis_size(TEXEL), lax.axis_size(LIGHT)
    share_rows = capacity // places
    counts = row_counts.reshape(1, texels)

    inputs = (tex_feat, light_feat, sketch)
    tiles, part = tile_call(0, *inputs)
    passing = across(part, 1)
    tiles, turned = tile_call(2, *inputs, tiles)
    tiles, part = tile_call(1, *inputs, tiles)
    staying = across(part, 1)
    passed = across(turned + passing, 2)
    tiles, part = tile_call(3, *inputs, tiles)
    quarter = part + staying + passed
    own, following, opposite, previous = quarter.reshape(4, share_rows, width)
    arrived, third = onward(opposite, 1), onward(previous, -1)
    share = own + third + onward(following + arrived, 1)

    square = (width, width)
    quarter = lax.all_gather(share, FAR, axis=0, tiled=True)
    near = across(quarter, 2)
    gram = on_core(gram_kernel, jax.ShapeDtypeStruct(square, F32), "gram_part")(counts, quarter)
    gram_rows = each_to_each(gram.reshape(texels, width // texels, width), TEXEL)
    gram_rows, near, quarter = lax.optimization_barrier((gram_rows, near, quarter))
    beyond, beside = across(near, 1), across(quarter, 1)
    gram_rows = sum_to_each(gram_rows, ("z1", "z0"))
    gram_rows = jnp.sum(gram_rows, axis=0)
    gram = each_to_each(jnp.broadcast_to(gram_rows, (texels, *gram_rows.shape)), TEXEL).reshape(square)

    lines, chips = width // texels, lax.axis_size(CHIP)
    basis, keep, send = on_core(
        basis_kernel,
        (
            jax.ShapeDtypeStruct((capacity, width), F32),
            jax.ShapeDtypeStruct((chips, lines, lights), F32),
            jax.ShapeDtypeStruct((chips, lines, lights), F32),
        ),
        "basis_and_coeffs",
        [pltpu.VMEM(square, F32)] * 3
        + [pltpu.VMEM((capacity, width), BF16), pltpu.VMEM((texels, lines, lights), F32)],
    )(counts, gram, beyond, beside, near, quarter, tiles)
    mine = keep + across_cores(send)
    coeffs = jnp.sum(each_to_each(mine, CHIP), axis=0)
    return basis, coeffs


def solution(mesh):
    fine = Mesh(np.asarray(mesh.devices).reshape(4, 4, 2, 2, 2, 2, 2), (*TEXEL, *LIGHT))
    placed = (P(TEXEL, None), P(LIGHT, None), P(LIGHT, None), P())
    return jax.shard_map(
        on_device, mesh=fine, in_specs=placed, out_specs=(P(TEXEL, None), P(TEXEL, LIGHT)), check_vma=False
    )
```

```python
import functools
import math

import jax
import jax.numpy as jnp
import numpy as np
from jax import lax
from jax.experimental import pallas as pl
from jax.experimental.pallas import tpu as pltpu
from jax.sharding import Mesh, PartitionSpec as P

F32 = jnp.float32
BF16 = jnp.bfloat16
CHIP = ("x", "y")
TEXEL = CHIP + ("core",)
FAR = ("z3", "z2")
LIGHT = FAR + ("z1", "z0")
HIGHEST = lax.Precision.HIGHEST
VMEM_LIMIT = 24 * 2**20


def sine_coefficients():
    angle = (np.arange(4000) + 0.5) * math.pi / 4000
    u = 0.125 * (1 + np.cos(angle)) + 1e-9
    w = 1.0
    basis = np.stack([u ** (2 * i + 1) for i in range(5)], axis=1)
    fit, *_ = np.linalg.lstsq(basis / w, np.sin(2 * math.pi * u) / w, rcond=None)
    return [float(c) for c in fit]


SINE = sine_coefficients()
ROUNDER = float(1.5 * 2**23)


def sine(x):
    turns = x * F32(1 / (2 * math.pi))
    part = turns - ((turns + F32(ROUNDER)) - F32(ROUNDER))
    part = jnp.maximum(jnp.minimum(part, F32(0.5) - part), F32(-0.5) - part)
    sq = part * part
    value = F32(SINE[4])
    for c in SINE[3::-1]:
        value = value * sq + F32(c)
    return value * part


def dot(a, b, contract, precision=None):
    return lax.dot_general(
        a, b, ((contract[0:1], contract[1:2]), ((), ())), precision=precision, preferred_element_type=F32
    )


VMEM = pl.BlockSpec(memory_space=pltpu.VMEM)


def on_core(kernel, out_shape, name, scratch=(), flops=10**9, aliases=None):
    call = lambda *operands: pl.pallas_call(
        kernel,
        out_shape=out_shape,
        in_specs=[VMEM] * len(operands),
        out_specs=jax.tree.map(lambda _: VMEM, out_shape),
        scratch_shapes=scratch,
        input_output_aliases=aliases or {},
        compiler_params=pltpu.CompilerParams(vmem_limit_bytes=VMEM_LIMIT),
        cost_estimate=pl.CostEstimate(flops=flops, bytes_accessed=2**20, transcendentals=0),
        name=name,
    )(*operands)
    return call


def quarter_of(order):
    low, second, core = (lax.axis_index(axis) for axis in ("z0", "z1", "core"))
    if order < 2:
        return 2 * (1 - low) + (second + core + 1 - order) % 2
    return 2 * low + (second + 1 - (order - 2)) % 2


def partner(place, reach):
    places, shift = lax.axis_size(LIGHT), lax.axis_index("core") * reach
    return (((place - shift + places) % places ^ reach) + shift) % places


def split(value):
    high = value.astype(BF16)
    return high, (value - high.astype(F32)).astype(BF16)


def dot_split(a, b, contract):
    (a_high, a_low), (b_high, b_low) = a, b
    return dot(a_high, b_high, contract) + (dot(a_high, b_low, contract) + dot(a_low, b_high, contract))


def tile_kernel(tex_ref, light_ref, sketch_ref, *refs, order, step=128):
    tile_ref, part_ref = refs[-2:]
    rows, groups = part_ref.shape[0], lax.axis_size(FAR)
    share = rows // groups
    first = quarter_of(order) * rows
    holder = lax.axis_index(LIGHT)
    if order < 2:
        holder = partner(holder, 1)
    if order % 2 == 0:
        holder = partner(holder, 2)
    holder = holder // (lax.axis_size(LIGHT) // groups)
    onward = 1 - 2 * lax.axis_index("core")
    for at in range(0, rows, step):
        tex = tex_ref[pl.ds(pl.multiple_of(first + at, step), step), :]
        tile = sine(dot(tex, light_ref[...], (1, 1))).astype(BF16)
        tile_ref[order * rows + at : order * rows + at + step, :] = tile
        part = dot(tile, sketch_ref[...], (1, 0))
        for i in range(step // share):
            turn = (onward * (at // share + i - holder) + groups) % groups
            part_ref[pl.ds(pl.multiple_of(turn * share, share), share), :] = part[i * share : (i + 1) * share, :]


def tile_call(order, tex, light, sketch, *tiles):
    rows, lights, width = tex.shape[0] // 4, light.shape[0], sketch.shape[1]
    return on_core(
        functools.partial(tile_kernel, order=order),
        (jax.ShapeDtypeStruct((tex.shape[0], lights), BF16), jax.ShapeDtypeStruct((rows, width), F32)),
        "tile_quarter",
        flops=2 * rows * lights * (tex.shape[1] + width),
        aliases={3: 0} if tiles else None,
    )(tex, light, sketch, *tiles)


def used(counts_ref, order, shape):
    texel = lax.broadcasted_iota(jnp.int32, counts_ref.shape, 1)
    count = jnp.sum(jnp.where(texel == lax.axis_index(TEXEL), counts_ref[...], 0), axis=1, keepdims=True)
    return lax.broadcasted_iota(jnp.int32, shape, 0) + quarter_of(order) * shape[0] < count


def gram_kernel(counts_ref, quarter_ref, gram_ref):
    parts = split(jnp.where(used(counts_ref, 3, quarter_ref.shape), quarter_ref[...], 0.0))
    gram_ref[...] = dot_split(parts, parts, (0, 0))


def invert_factor(gram, y_ref, a_ref, w_ref):
    size = gram.shape[0]
    row = lax.broadcasted_iota(jnp.int32, (size, size), 0)
    col = lax.broadcasted_iota(jnp.int32, (size, size), 1)

    def lower_half(rest):
        return jnp.where(row > col, rest, jnp.where(row == col, 0.5 * rest, 0.0))

    diagonal = jnp.where(row == col, gram, 0.0)
    across_columns = lax.rsqrt(jnp.sum(diagonal, axis=0, keepdims=True))
    down_rows = lax.rsqrt(jnp.sum(diagonal, axis=1, keepdims=True))
    unit = jnp.where(row == col, F32(1), F32(0))
    a_ref[...] = gram
    y_ref[...] = (unit - lower_half(gram * down_rows * across_columns - unit)) * across_columns

    def refine(exact):
        y = y_ref[...]
        if exact:
            parts = split(y)
            rest = dot_split(split(dot_split(parts, split(a_ref[...]), (1, 0))), parts, (1, 1)) - unit
            y_ref[...] = y - dot_split(split(lower_half(rest)), parts, (1, 0))
        else:
            rough = y.astype(BF16)
            rest = dot(dot(rough, a_ref[...].astype(BF16), (1, 0)).astype(BF16), rough, (1, 1)) - unit
            y_ref[...] = y - dot(lower_half(rest).astype(BF16), rough, (1, 0))
        return jnp.sum(rest * rest)

    def steps(exact, enough):
        return lax.while_loop(
            lambda state: (state[0] < 8) & (state[1] > enough),
            lambda state: (state[0] + 1, refine(exact)),
            (jnp.int32(0), F32(1)),
        )[1]

    steps(False, 1e-1)
    rest = steps(True, 4e-6)

    @pl.when(jnp.logical_not(rest <= 4e-6))
    def _():
        y_ref[...] = unit
        line = lax.broadcasted_iota(jnp.int32, (size, 1), 0)
        w_ref[...] = gram

        def eliminate(j, carry):
            work = w_ref[...]
            column = jnp.sum(jnp.where(col == j, work, 0.0), axis=1, keepdims=True)
            pivot = lax.rsqrt(jnp.sum(jnp.where(line == j, column, 0.0), axis=0, keepdims=True))
            top = w_ref[pl.ds(j, 1), :] * pivot
            top_y = y_ref[pl.ds(j, 1), :] * pivot
            factor = jnp.where(line > j, column * pivot, 0.0)
            w_ref[...] = work - factor * top
            y_ref[...] = jnp.where(line == j, top_y, y_ref[...] - factor * top_y)
            return carry

        lax.fori_loop(0, size, eliminate, 0)


def basis_kernel(counts_ref, gram_ref, *refs):
    quarter_refs, tile_ref = refs[:4], refs[4]
    basis_ref, keep_ref, send_ref, inverse_ref, a_ref, w_ref, half_ref, coeff_ref = refs[5:]
    total = jnp.sum(counts_ref[...].astype(F32), axis=1, keepdims=True)
    invert_factor(gram_ref[...] / total, inverse_ref, a_ref, w_ref)
    rows = basis_ref.shape[0] // 4
    inverse = split(inverse_ref[...])
    for order, ref in enumerate(quarter_refs):
        basis = jnp.where(used(counts_ref, order, ref.shape), dot_split(split(ref[...]), inverse, (1, 1)), 0.0)
        basis_ref[pl.ds(pl.multiple_of(quarter_of(order) * rows, rows), rows), :] = basis
        half_ref[order * rows : (order + 1) * rows, :] = basis.astype(BF16)
    coeffs = dot(half_ref[...], tile_ref[...], (0, 0))
    coeff_ref[...] = (coeffs * (1.0 / jnp.sqrt(total))).reshape(coeff_ref.shape)
    core = lax.axis_index("core")
    for i in range(keep_ref.shape[0]):
        keep_ref[i] = coeff_ref[2 * i + core]
        send_ref[i] = coeff_ref[2 * i + 1 - core]


def light_pairs(count, reach):
    pairs = []
    for core in range(2):
        shift = core * reach
        for z in range(count):
            pairs.append((core * count + z, core * count + ((((z - shift) % count) ^ reach) + shift) % count))
    return pairs


def across(value, reach):
    return lax.ppermute(value, ("core", *LIGHT), light_pairs(lax.axis_size(LIGHT), reach))


def onward(value, turn):
    count = lax.axis_size(LIGHT)
    pairs = [(c * count + z, c * count + (z + 4 * turn * (1 - 2 * c)) % count) for c in range(2) for z in range(count)]
    return lax.ppermute(value, ("core", *LIGHT), pairs)


def across_cores(value):
    return lax.ppermute(value, "core", [(0, 1), (1, 0)])


def each_to_each(parts, axes):
    return lax.all_to_all(parts, axes, 0, 0, tiled=True)


def sum_kernel(parts_ref, copies_ref):
    copies_ref[...] = jnp.broadcast_to(jnp.sum(parts_ref[...], axis=0, keepdims=True), copies_ref.shape)


def sum_to_each(parts, axes):
    copies = jax.ShapeDtypeStruct((lax.axis_size(axes), *parts.shape[1:]), parts.dtype)
    return each_to_each(on_core(sum_kernel, copies, "sum_and_repeat")(parts), axes)


def on_device(tex_feat, light_feat, sketch, row_counts):
    capacity, width = tex_feat.shape[0], sketch.shape[1]
    lights = light_feat.shape[0]
    texels, places = lax.axis_size(TEXEL), lax.axis_size(LIGHT)
    share_rows = capacity // places
    counts = row_counts.reshape(1, texels)

    inputs = (tex_feat, light_feat, sketch)
    tiles, part = tile_call(0, *inputs)
    passing = across(part, 1)
    tiles, turned = tile_call(2, *inputs, tiles)
    tiles, part = tile_call(1, *inputs, tiles)
    staying = across(part, 1)
    passed = across(turned + passing, 2)
    tiles, part = tile_call(3, *inputs, tiles)
    quarter = part + staying + passed
    own, following, opposite, previous = quarter.reshape(4, share_rows, width)
    arrived, third = onward(opposite, 1), onward(previous, -1)
    share = own + third + onward(following + arrived, 1)

    square = (width, width)
    quarter = lax.all_gather(share, FAR, axis=0, tiled=True)
    near = across(quarter, 2)
    gram = on_core(gram_kernel, jax.ShapeDtypeStruct(square, F32), "gram_part")(counts, quarter)
    gram_rows = each_to_each(gram.reshape(texels, width // texels, width), TEXEL)
    gram_rows, near, quarter = lax.optimization_barrier((gram_rows, near, quarter))
    beyond = across(near, 1)
    gram_rows = sum_to_each(gram_rows, ("z1", "z0"))
    gram_rows, quarter = lax.optimization_barrier((jnp.sum(gram_rows, axis=0), quarter))
    beside = across(quarter, 1)
    gram = each_to_each(jnp.broadcast_to(gram_rows, (texels, *gram_rows.shape)), TEXEL).reshape(square)

    lines, chips = width // texels, lax.axis_size(CHIP)
    basis, keep, send = on_core(
        basis_kernel,
        (
            jax.ShapeDtypeStruct((capacity, width), F32),
            jax.ShapeDtypeStruct((chips, lines, lights), F32),
            jax.ShapeDtypeStruct((chips, lines, lights), F32),
        ),
        "basis_and_coeffs",
        [pltpu.VMEM(square, F32)] * 3
        + [pltpu.VMEM((capacity, width), BF16), pltpu.VMEM((texels, lines, lights), F32)],
    )(counts, gram, beyond, beside, near, quarter, tiles)
    mine = keep + across_cores(send)
    coeffs = jnp.sum(each_to_each(mine, CHIP), axis=0)
    return basis, coeffs


def solution(mesh):
    fine = Mesh(np.asarray(mesh.devices).reshape(4, 4, 2, 2, 2, 2, 2), (*TEXEL, *LIGHT))
    placed = (P(TEXEL, None), P(LIGHT, None), P(LIGHT, None), P())
    return jax.shard_map(
        on_device, mesh=fine, in_specs=placed, out_specs=(P(TEXEL, None), P(TEXEL, LIGHT)), check_vma=False
    )
```

```python
import functools
import math

import jax
import jax.numpy as jnp
import numpy as np
from jax import lax
from jax.experimental import pallas as pl
from jax.experimental.pallas import tpu as pltpu
from jax.sharding import Mesh, PartitionSpec as P

F32 = jnp.float32
BF16 = jnp.bfloat16
CHIP = ("x", "y")
TEXEL = CHIP + ("core",)
FAR = ("z3", "z2")
LIGHT = FAR + ("z1", "z0")
HIGHEST = lax.Precision.HIGHEST
VMEM_LIMIT = 24 * 2**20


def sine_coefficients():
    angle = (np.arange(4000) + 0.5) * math.pi / 4000
    u = 0.125 * (1 + np.cos(angle)) + 1e-9
    w = 1.0
    basis = np.stack([u ** (2 * i + 1) for i in range(5)], axis=1)
    fit, *_ = np.linalg.lstsq(basis / w, np.sin(2 * math.pi * u) / w, rcond=None)
    return [float(c) for c in fit]


SINE = sine_coefficients()
ROUNDER = float(1.5 * 2**23)


def sine(x):
    turns = x * F32(1 / (2 * math.pi))
    part = turns - ((turns + F32(ROUNDER)) - F32(ROUNDER))
    part = jnp.maximum(jnp.minimum(part, F32(0.5) - part), F32(-0.5) - part)
    sq = part * part
    value = F32(SINE[4])
    for c in SINE[3::-1]:
        value = value * sq + F32(c)
    return value * part


def dot(a, b, contract, precision=None):
    return lax.dot_general(
        a, b, ((contract[0:1], contract[1:2]), ((), ())), precision=precision, preferred_element_type=F32
    )


VMEM = pl.BlockSpec(memory_space=pltpu.VMEM)


def on_core(kernel, out_shape, name, scratch=(), flops=10**9, aliases=None):
    call = lambda *operands: pl.pallas_call(
        kernel,
        out_shape=out_shape,
        in_specs=[VMEM] * len(operands),
        out_specs=jax.tree.map(lambda _: VMEM, out_shape),
        scratch_shapes=scratch,
        input_output_aliases=aliases or {},
        compiler_params=pltpu.CompilerParams(vmem_limit_bytes=VMEM_LIMIT),
        cost_estimate=pl.CostEstimate(flops=flops, bytes_accessed=2**20, transcendentals=0),
        name=name,
    )(*operands)
    return call


def quarter_of(order):
    low, second, core = (lax.axis_index(axis) for axis in ("z0", "z1", "core"))
    if order < 2:
        return 2 * (1 - low) + (second + core + 1 - order) % 2
    return 2 * low + (second + 1 - (order - 2)) % 2


def partner(place, reach):
    places, shift = lax.axis_size(LIGHT), lax.axis_index("core") * reach
    return (((place - shift + places) % places ^ reach) + shift) % places


def split(value):
    high = value.astype(BF16)
    return high, (value - high.astype(F32)).astype(BF16)


def dot_split(a, b, contract):
    (a_high, a_low), (b_high, b_low) = a, b
    return dot(a_high, b_high, contract) + (dot(a_high, b_low, contract) + dot(a_low, b_high, contract))


def tile_kernel(tex_ref, light_ref, sketch_ref, *refs, order, step=256, span=512):
    tile_ref, part_ref = refs[-2:]
    rows, groups = part_ref.shape[0], lax.axis_size(FAR)
    share = rows // groups
    first = quarter_of(order) * rows
    holder = lax.axis_index(LIGHT)
    if order < 2:
        holder = partner(holder, 1)
    if order % 2 == 0:
        holder = partner(holder, 2)
    holder = holder // (lax.axis_size(LIGHT) // groups)
    onward = 1 - 2 * lax.axis_index("core")
    for at in range(0, rows, step):
        tex = tex_ref[pl.ds(pl.multiple_of(first + at, step), step), :]
        part = None
        for to in range(0, light_ref.shape[0], span):
            tile = sine(dot(tex, light_ref[to : to + span, :], (1, 1))).astype(BF16)
            tile_ref[order * rows + at : order * rows + at + step, to : to + span] = tile
            product = dot(tile, sketch_ref[to : to + span, :], (1, 0))
            part = product if part is None else part + product
        for i in range(step // share):
            turn = (onward * (at // share + i - holder) + groups) % groups
            part_ref[pl.ds(pl.multiple_of(turn * share, share), share), :] = part[i * share : (i + 1) * share, :]


def tile_call(order, tex, light, sketch, *tiles):
    rows, lights, width = tex.shape[0] // 4, light.shape[0], sketch.shape[1]
    return on_core(
        functools.partial(tile_kernel, order=order),
        (jax.ShapeDtypeStruct((tex.shape[0], lights), BF16), jax.ShapeDtypeStruct((rows, width), F32)),
        "tile_quarter",
        flops=2 * rows * lights * (tex.shape[1] + width),
        aliases={3: 0} if tiles else None,
    )(tex, light, sketch, *tiles)


def used(counts_ref, order, shape):
    texel = lax.broadcasted_iota(jnp.int32, counts_ref.shape, 1)
    count = jnp.sum(jnp.where(texel == lax.axis_index(TEXEL), counts_ref[...], 0), axis=1, keepdims=True)
    return lax.broadcasted_iota(jnp.int32, shape, 0) + quarter_of(order) * shape[0] < count


def gram_kernel(counts_ref, quarter_ref, gram_ref):
    parts = split(jnp.where(used(counts_ref, 3, quarter_ref.shape), quarter_ref[...], 0.0))
    gram_ref[...] = dot_split(parts, parts, (0, 0))


def invert_factor(gram, y_ref, a_ref, w_ref):
    size = gram.shape[0]
    row = lax.broadcasted_iota(jnp.int32, (size, size), 0)
    col = lax.broadcasted_iota(jnp.int32, (size, size), 1)

    def lower_half(rest):
        return jnp.where(row > col, rest, jnp.where(row == col, 0.5 * rest, 0.0))

    diagonal = jnp.where(row == col, gram, 0.0)
    across_columns = lax.rsqrt(jnp.sum(diagonal, axis=0, keepdims=True))
    down_rows = lax.rsqrt(jnp.sum(diagonal, axis=1, keepdims=True))
    unit = jnp.where(row == col, F32(1), F32(0))
    a_ref[...] = gram
    y_ref[...] = (unit - lower_half(gram * down_rows * across_columns - unit)) * across_columns

    def refine(exact):
        y = y_ref[...]
        if exact:
            parts = split(y)
            rest = dot_split(split(dot_split(parts, split(a_ref[...]), (1, 0))), parts, (1, 1)) - unit
            y_ref[...] = y - dot_split(split(lower_half(rest)), parts, (1, 0))
        else:
            rough = y.astype(BF16)
            rest = dot(dot(rough, a_ref[...].astype(BF16), (1, 0)).astype(BF16), rough, (1, 1)) - unit
            y_ref[...] = y - dot(lower_half(rest).astype(BF16), rough, (1, 0))
        return jnp.sum(rest * rest)

    def steps(exact, enough):
        return lax.while_loop(
            lambda state: (state[0] < 8) & (state[1] > enough),
            lambda state: (state[0] + 1, refine(exact)),
            (jnp.int32(0), F32(1)),
        )[1]

    steps(False, 1e-1)
    rest = steps(True, 4e-6)

    @pl.when(jnp.logical_not(rest <= 4e-6))
    def _():
        y_ref[...] = unit
        line = lax.broadcasted_iota(jnp.int32, (size, 1), 0)
        w_ref[...] = gram

        def eliminate(j, carry):
            work = w_ref[...]
            column = jnp.sum(jnp.where(col == j, work, 0.0), axis=1, keepdims=True)
            pivot = lax.rsqrt(jnp.sum(jnp.where(line == j, column, 0.0), axis=0, keepdims=True))
            top = w_ref[pl.ds(j, 1), :] * pivot
            top_y = y_ref[pl.ds(j, 1), :] * pivot
            factor = jnp.where(line > j, column * pivot, 0.0)
            w_ref[...] = work - factor * top
            y_ref[...] = jnp.where(line == j, top_y, y_ref[...] - factor * top_y)
            return carry

        lax.fori_loop(0, size, eliminate, 0)


def basis_kernel(counts_ref, gram_ref, *refs):
    quarter_refs, tile_ref = refs[:4], refs[4]
    basis_ref, keep_ref, send_ref, inverse_ref, a_ref, w_ref, half_ref, coeff_ref = refs[5:]
    total = jnp.sum(counts_ref[...].astype(F32), axis=1, keepdims=True)
    invert_factor(gram_ref[...] / total, inverse_ref, a_ref, w_ref)
    rows = basis_ref.shape[0] // 4
    inverse = split(inverse_ref[...])
    for order, ref in enumerate(quarter_refs):
        basis = jnp.where(used(counts_ref, order, ref.shape), dot_split(split(ref[...]), inverse, (1, 1)), 0.0)
        basis_ref[pl.ds(pl.multiple_of(quarter_of(order) * rows, rows), rows), :] = basis
        half_ref[order * rows : (order + 1) * rows, :] = basis.astype(BF16)
    coeffs = dot(half_ref[...], tile_ref[...], (0, 0))
    coeff_ref[...] = (coeffs * (1.0 / jnp.sqrt(total))).reshape(coeff_ref.shape)
    core = lax.axis_index("core")
    for i in range(keep_ref.shape[0]):
        keep_ref[i] = coeff_ref[2 * i + core]
        send_ref[i] = coeff_ref[2 * i + 1 - core]


def light_pairs(count, reach):
    pairs = []
    for core in range(2):
        shift = core * reach
        for z in range(count):
            pairs.append((core * count + z, core * count + ((((z - shift) % count) ^ reach) + shift) % count))
    return pairs


def across(value, reach):
    return lax.ppermute(value, ("core", *LIGHT), light_pairs(lax.axis_size(LIGHT), reach))


def onward(value, turn):
    count = lax.axis_size(LIGHT)
    pairs = [(c * count + z, c * count + (z + 4 * turn * (1 - 2 * c)) % count) for c in range(2) for z in range(count)]
    return lax.ppermute(value, ("core", *LIGHT), pairs)


def across_cores(value):
    return lax.ppermute(value, "core", [(0, 1), (1, 0)])


def each_to_each(parts, axes):
    return lax.all_to_all(parts, axes, 0, 0, tiled=True)


def sum_kernel(parts_ref, copies_ref):
    copies_ref[...] = jnp.broadcast_to(jnp.sum(parts_ref[...], axis=0, keepdims=True), copies_ref.shape)


def sum_to_each(parts, axes):
    copies = jax.ShapeDtypeStruct((lax.axis_size(axes), *parts.shape[1:]), parts.dtype)
    return each_to_each(on_core(sum_kernel, copies, "sum_and_repeat")(parts), axes)


def on_device(tex_feat, light_feat, sketch, row_counts):
    capacity, width = tex_feat.shape[0], sketch.shape[1]
    lights = light_feat.shape[0]
    texels, places = lax.axis_size(TEXEL), lax.axis_size(LIGHT)
    share_rows = capacity // places
    counts = row_counts.reshape(1, texels)

    inputs = (tex_feat, light_feat, sketch)
    tiles, part = tile_call(0, *inputs)
    passing = across(part, 1)
    tiles, turned = tile_call(2, *inputs, tiles)
    tiles, part = tile_call(1, *inputs, tiles)
    staying = across(part, 1)
    passed = across(turned + passing, 2)
    tiles, part = tile_call(3, *inputs, tiles)
    quarter = part + staying + passed
    own, following, opposite, previous = quarter.reshape(4, share_rows, width)
    arrived, third = onward(opposite, 1), onward(previous, -1)
    share = own + third + onward(following + arrived, 1)

    square = (width, width)
    quarter = lax.all_gather(share, FAR, axis=0, tiled=True)
    near = across(quarter, 2)
    gram = on_core(gram_kernel, jax.ShapeDtypeStruct(square, F32), "gram_part")(counts, quarter)
    gram_rows = each_to_each(gram.reshape(texels, width // texels, width), TEXEL)
    gram_rows, near, quarter = lax.optimization_barrier((gram_rows, near, quarter))
    beyond, beside = across(near, 1), across(quarter, 1)
    gram_rows = sum_to_each(gram_rows, ("z1", "z0"))
    gram_rows = jnp.sum(gram_rows, axis=0)
    gram = each_to_each(jnp.broadcast_to(gram_rows, (texels, *gram_rows.shape)), TEXEL).reshape(square)

    lines, chips = width // texels, lax.axis_size(CHIP)
    basis, keep, send = on_core(
        basis_kernel,
        (
            jax.ShapeDtypeStruct((capacity, width), F32),
            jax.ShapeDtypeStruct((chips, lines, lights), F32),
            jax.ShapeDtypeStruct((chips, lines, lights), F32),
        ),
        "basis_and_coeffs",
        [pltpu.VMEM(square, F32)] * 3
        + [pltpu.VMEM((capacity, width), BF16), pltpu.VMEM((texels, lines, lights), F32)],
    )(counts, gram, beyond, beside, near, quarter, tiles)
    mine = keep + across_cores(send)
    coeffs = jnp.sum(each_to_each(mine, CHIP), axis=0)
    return basis, coeffs


def solution(mesh):
    fine = Mesh(np.asarray(mesh.devices).reshape(4, 4, 2, 2, 2, 2, 2), (*TEXEL, *LIGHT))
    placed = (P(TEXEL, None), P(LIGHT, None), P(LIGHT, None), P())
    return jax.shard_map(
        on_device, mesh=fine, in_specs=placed, out_specs=(P(TEXEL, None), P(TEXEL, LIGHT)), check_vma=False
    )
```
